32 devices in a mesh: row: 4 (over y, x), col: 8 (over z, core).
Axes of the slice: x: 2, y: 2, z: 4, core: 2. Of those that a mesh axis runs over, the one named last changes fastest.
Arguments:
- fitting: bfloat16 [64, 512, 256], P(('row', 'col')), may hold values from -6 to 6
- coefficients: bfloat16 [16, 16, 6, 256, 128], P('row', 'col'), may hold values from -0.375 to 0.375
- amplitudes: bfloat16 [16, 16, 4096], P('row', 'col'), may hold values from -6 to 6
- intersections: bfloat16 [16, 16, 8, 4096], P('row', 'col'), may hold values from -0.33 to 1.33
- virtual_energy: float32 [16, 16, 64], P('row', 'col'), may hold values from 0.2 to 2
- occupied_energy: float32 [16], replicated, may hold values from -1.5 to -0.3
- kept_count: int32 [16, 16], P('row', 'col'), may hold values from 16 to 64
- orbital_atoms: int32 [16, 3], replicated, may hold values from 0 to 63, as said below
- fock_partner: int32 [16, 4], replicated, may hold values from 0 to 15, as said below
- fock_value: float32 [16, 4], replicated, may hold values from -3 to 3
Outputs:
- residual: float32 [16, 16, 4096], P('row', 'col')
The draws below stay inside these ranges and needn't reach their ends.
Inputs may be any that keep to these rules, and one draw needn't show every extreme that they name: `orbital_atoms`: the 3 atoms of orbital i are different and lie in [(i // 4) * 16, (i // 4 + 1) * 16). fock_partner[i, n] differs from i by at most 2.
All inputs are finite; a program needn't handle non-finite values.
Results may differ from the reference program's by a relative error of at most 0.0029.
Values may be sent and summed in bfloat16 or wider, within the bound.
No kernel may reach another device: no remote copies, remote signals or barrier semaphores. Data moves between devices by JAX's collectives and lax.ppermute only.
A program may use at most 128 MiB of HBM per device.

```python
import math
import jax
import jax.numpy as jnp
from jax import lax

AUX = 512
PAO = 256
NPNO = 64
DOMAIN = 3
PARTNERS = 4
I_DEV = 4
NOCC = 16
J_DEV = 2
NATOMS = 64
ROW_ATOMS = 16


def draw_intersections(key, part):
    first, second = jax.random.split(key)
    diagonal = jax.random.uniform(first, (NOCC, NOCC, 2 * PARTNERS, NPNO), jnp.float32, 0.7, 1.0)
    noise = jnp.clip(jax.random.normal(second, (NOCC, NOCC, 2 * PARTNERS, NPNO, NPNO), jnp.float32), -4.0, 4.0) * 0.08
    identity = jnp.eye(NPNO, dtype=jnp.float32)
    whole = noise + diagonal[..., :, None] * identity
    return whole.reshape(NOCC, NOCC, 2 * PARTNERS, NPNO * NPNO).astype(jnp.bfloat16)


def draw_orbital_atoms(key, part):
    scores = jax.random.randint(key, (NOCC, ROW_ATOMS), 0, 1 << 20) * ROW_ATOMS + jnp.arange(ROW_ATOMS, dtype=jnp.int32)[None, :]
    chosen = jnp.argsort(scores, axis=1, stable=True)[:, :DOMAIN].astype(jnp.int32)
    base = jnp.arange(NOCC, dtype=jnp.int32) // I_DEV * ROW_ATOMS
    return (chosen + base[:, None]).astype(jnp.int32)


def draw_fock_partner(key, part):
    first, second = jax.random.split(key)
    reach = jax.random.randint(first, (NOCC, PARTNERS), 1, J_DEV + 1)
    direction = 2 * jax.random.randint(second, (NOCC, PARTNERS), 0, 2) - 1
    target = jnp.arange(NOCC, dtype=jnp.int32)[:, None] + reach * direction
    target = jnp.where(target < 0, -target, target)
    target = jnp.where(target > NOCC - 1, 2 * (NOCC - 1) - target, target)
    return target.astype(jnp.int32)


def plant(entries, key, smallest, top_value):
    longest = entries.shape.index(max(entries.shape))
    spots = []
    for shift in (0, 1):
        where = [jax.random.randint(jax.random.fold_in(key, axis), (), 0, length) for axis, length in enumerate(entries.shape)]
        where[longest] = (where[longest] + shift) % entries.shape[longest]
        spots.append(tuple(where))
    return entries.at[spots[0]].set(smallest).at[spots[1]].set(top_value)


def block_levels(rng, dims, cuts, low, top_value):
    gain, own = 1.0, jax.random.fold_in(rng, 6)
    for dim, blocks in cuts:
        draws = jnp.exp(jax.random.uniform(jax.random.fold_in(own, dim), (blocks,), jnp.float32, low / len(cuts), top_value / len(cuts)))
        gain = gain * jnp.repeat(draws, dims[dim] // blocks).reshape([-1 if axis == dim else 1 for axis in range(len(dims))])
    return gain


def scatter_about(stream_key, dims, width, bound, cuts=(), kind=jnp.bfloat16):
    factor_of = block_levels(stream_key, dims, cuts, -0.22, 0.18) if cuts else 1.0
    entries = jax.random.normal(stream_key, dims, jnp.float32) * width * factor_of
    return jnp.minimum(jnp.maximum(entries, -bound), bound).astype(kind)


def setup_inputs(seed: int = 0) -> dict:
    key_of = jax.random.split(jax.random.key(seed), 11)
    fitting = scatter_about(key_of[0], (NATOMS, AUX, PAO), 1.0, 6.0, ((0, 32),))
    coefficients = scatter_about(key_of[1], (NOCC, NOCC, 2 * DOMAIN, PAO, 2 * NPNO), PAO ** -0.5, 0.375, ((0, 4), (1, 8)))
    amplitudes = scatter_about(key_of[2], (NOCC, NOCC, NPNO * NPNO), 1.0, 6.0, ((0, 4), (1, 8)))
    intersections = draw_intersections(jax.random.fold_in(key_of[10], 71), 0)
    virtual_energy = jnp.clip(jnp.exp(math.log(2.0) - 2.3025851 * jax.random.uniform(key_of[4], (NOCC, NOCC, NPNO), jnp.float32) ** block_levels(key_of[4], (NOCC, NOCC, NPNO), ((0, 4), (1, 8)), -0.2, 0.2)), 0.2, 2.0)
    occupied_energy = jnp.clip(jax.random.uniform(key_of[5], (NOCC,), jnp.float32, -1.5, -0.3), -1.5, -0.3)
    kept_count = plant(jax.random.randint(key_of[6], (NOCC, NOCC), NPNO // 4, NPNO + 1), jax.random.fold_in(key_of[6], 1), NPNO // 4, NPNO).astype(jnp.int32)
    orbital_atoms = draw_orbital_atoms(jax.random.fold_in(key_of[10], 71), 0)
    fock_partner = draw_fock_partner(jax.random.fold_in(key_of[10], 71), 0)
    fock_value = scatter_about(key_of[9], (NOCC, PARTNERS), 0.5, 3.0, (), jnp.float32)
    return dict(fitting=fitting, coefficients=coefficients, amplitudes=amplitudes, intersections=intersections, virtual_energy=virtual_energy, occupied_energy=occupied_energy, kept_count=kept_count, orbital_atoms=orbital_atoms, fock_partner=fock_partner, fock_value=fock_value)


def reference(fitting, coefficients, amplitudes, intersections, virtual_energy, occupied_energy, kept_count, orbital_atoms, fock_partner, fock_value):
    highest = lax.Precision.HIGHEST
    total = amplitudes.shape[0]
    matrices = amplitudes.reshape(total, total, NPNO, NPNO)
    column_fit = fitting[orbital_atoms].astype(jnp.float32)
    levels = jnp.arange(NPNO, dtype=jnp.int32)

    def one_row(orbital):
        row_fit = fitting[orbital_atoms[orbital]].astype(jnp.float32)
        mapping = coefficients[orbital].astype(jnp.float32)
        own_side = jnp.einsum("sap,jspq->jsaq", row_fit, mapping[:, :DOMAIN], precision=highest).astype(jnp.bfloat16).astype(jnp.float32)
        other_side = jnp.einsum("jsap,jspq->jsaq", column_fit, mapping[:, DOMAIN:], precision=highest).astype(jnp.bfloat16).astype(jnp.float32)
        exchange_part = jnp.einsum("jsaq,jsar->jqr", own_side[..., :NPNO], own_side[..., NPNO:], precision=highest)
        exchange_part = exchange_part + jnp.einsum("jsaq,jsar->jqr", other_side[..., :NPNO], other_side[..., NPNO:], precision=highest)
        exchange_part = exchange_part * ((2 * DOMAIN * AUX) ** -0.5)
        from_rows = jnp.transpose(matrices[fock_partner[orbital]], (1, 0, 2, 3))
        from_columns = matrices[orbital][fock_partner]
        partners = jnp.concatenate([from_rows, from_columns], axis=1).astype(jnp.float32)
        intersection_mats = intersections[orbital].reshape(total, 2 * PARTNERS, NPNO, NPNO).astype(jnp.float32)
        half = jnp.einsum("jnab,jnbc->jnac", intersection_mats, partners, precision=highest).astype(jnp.bfloat16)
        sandwich = jnp.einsum("jnac,jndc->jnad", half.astype(jnp.float32), intersection_mats, precision=highest)
        own_weight = jnp.broadcast_to(fock_value[orbital][None, :], (total, PARTNERS))
        weights = jnp.concatenate([own_weight, fock_value], axis=1)
        coupling = jnp.einsum("jn,jnad->jad", weights, sandwich, precision=highest)
        energies = virtual_energy[orbital]
        shift = energies[:, :, None] + energies[:, None, :] - occupied_energy[orbital] - occupied_energy[:, None, None]
        result = exchange_part + shift * matrices[orbital].astype(jnp.float32) - coupling
        count = kept_count[orbital][:, None, None]
        keep = (levels[None, :, None] < count) & (levels[None, None, :] < count)
        return jnp.where(keep, result, jnp.zeros_like(result)).reshape(total, NPNO * NPNO)

    return lax.map(one_row, jnp.arange(total, dtype=jnp.int32))
```

```python
import functools

import jax
import jax.numpy as jnp
from jax import lax
from jax.experimental import pallas as pl
from jax.experimental.pallas import tpu as pltpu
from jax.sharding import PartitionSpec as P

F32 = jnp.float32
BF16 = jnp.bfloat16
EXTRA = 16
VMEM = pl.BlockSpec(memory_space=pltpu.VMEM)
SMEM = pl.BlockSpec(memory_space=pltpu.SMEM)


def dot(a, b):
    return jnp.dot(a, b, preferred_element_type=F32)


def dot_nt(a, b):
    return lax.dot_general(a, b, (((1,), (1,)), ((), ())), preferred_element_type=F32)


def square_iota(n):
    return (
        lax.broadcasted_iota(jnp.int32, (n, n), 0),
        lax.broadcasted_iota(jnp.int32, (n, n), 1),
    )


def pack_kernel(fit_ref, out_ref):
    half = fit_ref.shape[2] // 2
    row, col = square_iota(half)
    place = lax.broadcasted_iota(jnp.int32, (EXTRA, half), 0)
    for atom in range(fit_ref.shape[0]):
        fit = fit_ref[atom]
        metric = lax.dot_general(fit, fit, (((0,), (0,)), ((), ())), preferred_element_type=F32)
        first, second = metric[:half, :half], metric[half:, half:]
        out_ref[atom, :half] = metric[:half, half:].astype(BF16)
        out_ref[atom, half : 2 * half] = jnp.where(row <= col, first, second).astype(BF16)
        lines = [jnp.sum(jnp.where(row == col, m, 0.0), axis=0, keepdims=True) for m in (first, second)]
        high = [line.astype(BF16).astype(F32) for line in lines]
        extra = jnp.where(
            place == 0,
            high[1],
            jnp.where(
                place == 1,
                lines[0] - high[0],
                jnp.where(place == 2, lines[1] - high[1], 0.0),
            ),
        )
        out_ref[atom, 2 * half :] = extra.astype(BF16)


def unpack(packed, metric_ref):
    half = packed.shape[1]
    row, col = square_iota(half)
    corner = packed[:half]
    both = packed[half : 2 * half].astype(F32)
    extra = packed[2 * half :].astype(F32)
    turned = both.T
    metric_ref[:half, :half] = jnp.where(row <= col, both, turned).astype(BF16)
    metric_ref[:half, half:] = corner
    metric_ref[half:, :half] = corner.astype(F32).T.astype(BF16)
    metric_ref[half:, half:] = jnp.where(
        row > col, both, jnp.where(row == col, extra[0:1], turned)
    ).astype(BF16)
    return jnp.concatenate([extra[1:2], extra[2:3]], axis=1)


def ring_order(units):
    return [0] + list(range(1, units, 2)) + list(range(units - units % 2 - (0 if units % 2 else 2), 0, -2))


def ring_place(unit, units):
    return jnp.where(unit % 2 == 1, (unit + 1) // 2, (units - unit // 2) % units)


def pick_place(atom, row_place, col_place, cores, units, held):
    label = jnp.clip(atom - row_place * (units * cores * held), 0, units * cores * held - 1)
    owner, slot = label // held, label % held
    turn = (ring_place(col_place // cores, units) - ring_place(owner // cores, units) + units) % units
    side = (col_place % cores - owner % cores + cores) % cores
    return (turn * cores + side) * held + slot


def collect(buffers, all_ref):
    held = buffers[0].shape[0]
    for index, buffer in enumerate(buffers):
        all_ref[index * held : (index + 1) * held] = buffer[...]


def select_kernel(cores, units, pieces, atoms_ref, *refs):
    count = units * cores
    buffers, outs, all_ref = refs[:count], refs[count:-1], refs[-1]
    held = buffers[0].shape[0]
    row_place, col_place = lax.axis_index("row"), lax.axis_index("col")
    domain = atoms_ref.shape[0]
    columns = sum(pieces) // domain
    collect(buffers, all_ref)
    targets = [(out, n) for out in outs for n in range(out.shape[0])]
    for index, (out, n) in enumerate(targets):
        atom = atoms_ref[index % domain, col_place * columns + index // domain]
        place = pick_place(atom, row_place, col_place, cores, units, held)
        out[n] = all_ref[place]


def neighbour_place(place, turn):
    return jnp.where(turn == 0, 0, jnp.where((place + turn) == jnp.bitwise_xor(place, 1), 1, 2))


def couple_kernel(
    partner_ref, value_ref, occupied_ref, coef_ref, inter_ref, virtual_ref, *refs,
):
    blocks = refs[:5]
    base_ref, turned_ref, flat_ref, wide_ref, mats_ref, inters_ref = refs[5:]
    row_count, column_count, terms, size = inter_ref.shape
    npno = base_ref.shape[2]
    lanes = 2 * npno
    chunks = size // lanes
    domain = coef_ref.shape[2] // 2
    partners = terms // 2
    row_place, col_place = lax.axis_index("row"), lax.axis_index("col")
    first_row = row_place * row_count
    first_col = col_place * column_count

    def square(lines):
        wide_ref[pl.ds(0, chunks, 2), :] = lines
        wide_ref[pl.ds(1, chunks, 2), :] = pltpu.roll(lines, npno, 1)
        return wide_ref[:, :npno].astype(BF16)

    for index, block in enumerate(blocks):

        def one_block(i, carry, index=index, block=block):
            for q in range(chunks):
                flat_ref[q, :column_count] = block[i, :, q * lanes : (q + 1) * lanes].astype(F32)
            for j in range(column_count):
                mats_ref[index * row_count + i, j] = square(flat_ref[:, j, :])
            return carry

        lax.fori_loop(0, row_count, one_block, 0)

    def one_row(i, carry):
        for j in range(column_count):
            for q in range(chunks):
                flat_ref[q] = inter_ref[i, j, :, q * lanes : (q + 1) * lanes].astype(F32)
            for n in range(terms):
                inters_ref[n] = square(flat_ref[:, n, :])
            total = jnp.zeros((npno, npno), F32)
            for n in range(terms):
                if n < partners:
                    away = partner_ref[n, first_row + i] - first_row + row_count
                    turn = away // row_count - 1
                    index = neighbour_place(row_place, turn) * row_count + away % row_count
                    weight = value_ref[n, first_row + i]
                    partner = mats_ref[index, j]
                else:
                    away = partner_ref[n - partners, first_col + j] - first_col + column_count
                    turn = away // column_count - 1
                    index = neighbour_place(col_place, turn)
                    index = jnp.where(index == 0, 0, index + 2) * row_count + i
                    weight = value_ref[n - partners, first_col + j]
                    partner = mats_ref[index, away % column_count]
                inter = inters_ref[n]
                half = dot(inter, partner).astype(BF16)
                total = total + weight * dot_nt(half, inter)
            levels = jnp.broadcast_to(virtual_ref[i, pl.ds(j, 1)], (npno, npno))
            shift = levels + levels.T - occupied_ref[first_row + i] - occupied_ref[first_col + j]
            base_ref[i, j] = shift * mats_ref[i, j].astype(F32) - total
            for s in range(domain):
                turned = coef_ref[i, j, domain + s].T
                turned_ref[j, s, pl.ds(pl.multiple_of(i * npno, npno), npno)] = turned[:npno]
        return carry

    lax.fori_loop(0, row_count, one_row, 0)


def row_kernel(cores, units, scale, atoms_ref, coef_ref, base_ref, *refs):
    count = units * cores
    buffers = refs[:count]
    out_ref, all_ref, metric_ref = refs[count:]
    held = buffers[0].shape[0]
    row_count, column_count = coef_ref.shape[:2]
    domain = coef_ref.shape[2] // 2
    npno = base_ref.shape[2]
    row_place, col_place = lax.axis_index("row"), lax.axis_index("col")
    collect(buffers, all_ref)

    def one_row(i, carry):
        totals = [None] * column_count
        for s in range(domain):
            atom = atoms_ref[s, row_place * row_count + i]
            place = pick_place(atom, row_place, col_place, cores, units, held)
            low = unpack(all_ref[place], metric_ref)
            left = jnp.concatenate([coef_ref[i, j, s].T[:npno] for j in range(column_count)], axis=0)
            product = dot(left, metric_ref[...]) + left.astype(F32) * low
            product = product.astype(BF16)
            for j in range(column_count):
                part = dot(product[j * npno : (j + 1) * npno], coef_ref[i, j, s])
                totals[j] = part if s == 0 else totals[j] + part
        for j in range(column_count):
            out_ref[i, j] = base_ref[i, j] + totals[j][:, npno:] * scale
        return carry

    lax.fori_loop(0, row_count, one_row, 0)


def column_kernel(routes, pieces, scale, kept_ref, coef_ref, turned_ref, base_ref, *refs):
    own_count = len(pieces)
    own_pieces = refs[:own_count]
    arrived = refs[own_count : own_count + len(routes)]
    out_ref, packed_ref, metric_ref, wide_ref, flat_ref = refs[own_count + len(routes) :]
    row_count, column_count = coef_ref.shape[:2]
    domain = coef_ref.shape[2] // 2
    npno = base_ref.shape[2]
    lanes = 2 * npno
    source = lax.axis_index("col") * column_count // row_count
    away = jnp.bitwise_xor(lax.axis_index("row"), source)
    starts = [sum(pieces[:p]) for p in range(own_count)]

    for p in range(own_count):

        @pl.when(away == 0)
        def _(p=p):
            packed_ref[starts[p] : starts[p] + pieces[p]] = own_pieces[p][...]

    for (p, takers), buffer in zip(routes, arrived):
        meant = functools.reduce(jnp.logical_or, [away == taker for taker in takers])

        @pl.when(meant)
        def _(p=p, buffer=buffer):
            packed_ref[starts[p] : starts[p] + pieces[p]] = buffer[...]

    totals = {}
    for index in range(column_count * domain):
        j, s = index // domain, index % domain
        low = unpack(packed_ref[index], metric_ref)
        left = turned_ref[j, s]
        product = dot(left, metric_ref[...]) + left.astype(F32) * low
        product = product.astype(BF16)
        for i in range(row_count):
            part = dot(product[i * npno : (i + 1) * npno], coef_ref[i, j, domain + s])
            totals[i, j] = part if s == 0 else totals[i, j] + part
    row, col = square_iota(npno)
    lane = lax.broadcasted_iota(jnp.int32, (npno // 2, lanes), 1)
    for i in range(row_count):
        for j in range(column_count):
            result = base_ref[i, j] + totals[i, j][:, npno:] * scale
            kept = kept_ref[j, i]
            result = jnp.where((row < kept) & (col < kept), result, 0.0)
            wide_ref[:, :npno] = result
            even = wide_ref[pl.ds(0, npno // 2, 2), :]
            odd = wide_ref[pl.ds(1, npno // 2, 2), :]
            flat_ref[i, j] = jnp.where(lane < npno, even, pltpu.roll(odd, npno, 1))
    for i in range(row_count):
        for q in range(npno // 2):
            out_ref[i, :, q * lanes : (q + 1) * lanes] = flat_ref[i, :, q, :]


def call(kernel, out_shape, in_specs, out_specs, scratch, name, flops, moved):
    return pl.pallas_call(
        kernel,
        out_shape=out_shape,
        in_specs=in_specs,
        out_specs=out_specs,
        scratch_shapes=scratch,
        compiler_params=pltpu.CompilerParams(vmem_limit_bytes=48 * 2**20),
        cost_estimate=pl.CostEstimate(flops=flops, bytes_accessed=moved, transcendentals=0),
        name=name,
    )


def swapped(block, axis, first):
    size = lax.axis_size(axis)
    pairs = [(n, n + 1) for n in range(first, size - 1, 2)]
    return lax.ppermute(block, axis, pairs + [(b, a) for a, b in pairs])


def gather_metrics(packed, cores, units):
    order = ring_order(units)
    forward = [
        (order[n] * cores + k, order[(n + 1) % units] * cores + k)
        for n in range(units)
        for k in range(cores)
    ]
    backward = [(b, a) for a, b in forward]
    turns = [packed] + [None] * (units - 1)
    up = down = packed
    for step in range(1, units // 2 + 1):
        up = lax.ppermute(up, "col", forward)
        turns[step] = up
        if units - step > units // 2:
            down = lax.ppermute(down, "col", backward)
            turns[units - step] = down
    buffers = []
    for turn in turns:
        buffers.append(turn)
        for side in range(1, cores):
            swap = [
                (u * cores + k, u * cores + (k + side) % cores)
                for u in range(units)
                for k in range(cores)
            ]
            buffers.append(lax.ppermute(turn, "col", swap))
    return buffers


def spread(own_pieces, sources):
    rows, columns = lax.axis_size("row"), len(sources)
    bits = rows.bit_length() - 1
    assert rows == 1 << bits
    held = [{0: own_pieces[p]} for p in range(bits)]
    reached = [{0: [0]} for p in range(bits)]
    routes, arrived = [], []
    for step in range(bits):
        for p in range(bits):
            bit = 1 << ((p + step) % bits)
            got, takers = [], []
            for since in sorted(held[p]):
                pairs = [
                    ((sources[c] ^ away) * columns + c, (sources[c] ^ away ^ bit) * columns + c)
                    for c in range(columns)
                    for away in reached[p][since]
                ]
                got.append(lax.ppermute(held[p][since], ("row", "col"), pairs))
                takers.append([away ^ bit for away in reached[p][since]])
            for block, who in zip(got, takers):
                routes.append((p, who))
                arrived.append(block)
                key = len(held[p])
                held[p][key] = block
                reached[p][key] = who
    return routes, arrived


def on_device(
    fitting,
    coefficients,
    amplitudes,
    intersections,
    virtual_energy,
    occupied_energy,
    kept_count,
    orbital_atoms,
    fock_partner,
    fock_value,
):
    row_count, column_count = amplitudes.shape[:2]
    held, aux, pao = fitting.shape
    domain = orbital_atoms.shape[1]
    npno = virtual_energy.shape[2]
    terms = intersections.shape[2]
    rows, columns = lax.axis_size("row"), lax.axis_size("col")
    cores = row_count // column_count
    units = columns // cores
    scale = (2 * domain * aux) ** (-0.5)
    depth = pao + EXTRA
    half = pao // 2

    packed = call(
        pack_kernel,
        jax.ShapeDtypeStruct((held, depth, half), BF16),
        [VMEM],
        VMEM,
        [],
        "pack_metric",
        2 * held * aux * pao * pao,
        fitting.size * 2,
    )(fitting)
    buffers = gather_metrics(packed, cores, units)

    blocks = [amplitudes] + [
        swapped(amplitudes, axis, first) for axis in ("row", "col") for first in (0, 1)
    ]
    chunks = npno // 2
    base, turned = call(
        couple_kernel,
        (
            jax.ShapeDtypeStruct((row_count, column_count, npno, npno), F32),
            jax.ShapeDtypeStruct((column_count, domain, row_count * npno, pao), BF16),
        ),
        [SMEM] * 3 + [VMEM] * (3 + len(blocks)),
        (VMEM, VMEM),
        [
            pltpu.VMEM((chunks, terms, 2 * npno), F32),
            pltpu.VMEM((npno, 2 * npno), F32),
            pltpu.VMEM((len(blocks) * row_count, column_count, npno, npno), BF16),
            pltpu.VMEM((terms, npno, npno), BF16),
        ],
        "couple",
        4 * row_count * column_count * terms * npno**3,
        intersections.size * 4 + coefficients.size,
    )(fock_partner.T, fock_value.T, occupied_energy, coefficients, intersections, virtual_energy, *blocks)

    bits = rows.bit_length() - 1
    wanted = column_count * domain
    pieces = [wanted * (p + 1) // bits - wanted * p // bits for p in range(bits)]
    own_pieces = call(
        functools.partial(select_kernel, cores, units, pieces),
        tuple(jax.ShapeDtypeStruct((n, depth, half), BF16) for n in pieces),
        [SMEM] + [VMEM] * len(buffers),
        (VMEM,) * bits,
        [pltpu.VMEM((len(buffers) * held, depth, half), BF16)],
        "select_column_atoms",
        0,
        wanted * depth * half * 4,
    )(orbital_atoms.T, *buffers)
    sources = [c * column_count // row_count for c in range(columns)]
    routes, arrived = spread(own_pieces, sources)

    base = call(
        functools.partial(row_kernel, cores, units, scale),
        jax.ShapeDtypeStruct(base.shape, F32),
        [SMEM] + [VMEM] * (2 + len(buffers)),
        VMEM,
        [
            pltpu.VMEM((len(buffers) * held, depth, half), BF16),
            pltpu.VMEM((pao, pao), BF16),
        ],
        "row_exchange",
        2 * row_count * column_count * domain * pao * npno * (pao + npno),
        coefficients.size,
    )(orbital_atoms.T, coefficients, base, *buffers)

    return call(
        functools.partial(column_kernel, routes, pieces, scale),
        jax.ShapeDtypeStruct(amplitudes.shape, F32),
        [SMEM] + [VMEM] * (3 + bits + len(arrived)),
        VMEM,
        [
            pltpu.VMEM((wanted, depth, half), BF16),
            pltpu.VMEM((pao, pao), BF16),
            pltpu.VMEM((npno, 2 * npno), F32),
            pltpu.VMEM((row_count, column_count, npno // 2, 2 * npno), F32),
        ],
        "column_exchange",
        2 * row_count * column_count * domain * pao * npno * (pao + npno),
        coefficients.size,
    )(kept_count.T, coefficients, turned, base, *own_pieces, *arrived)


def solution(mesh):
    placed = (
        P(("row", "col"), None, None),
        P("row", "col", None, None, None),
        P("row", "col", None),
        P("row", "col", None, None),
        P("row", "col", None),
        P(),
        P("row", "col"),
        P(),
        P(),
        P(),
    )
    return jax.shard_map(
        on_device, mesh=mesh, in_specs=placed, out_specs=P("row", "col", None), check_vma=False
    )
```

```python
import functools

import jax
import jax.numpy as jnp
from jax import lax
from jax.experimental import pallas as pl
from jax.experimental.pallas import tpu as pltpu
from jax.sharding import PartitionSpec as P

F32 = jnp.float32
BF16 = jnp.bfloat16
EXTRA = 16
VMEM = pl.BlockSpec(memory_space=pltpu.VMEM)
SMEM = pl.BlockSpec(memory_space=pltpu.SMEM)
HBM = pl.BlockSpec(memory_space=pltpu.HBM)
ANY = pl.BlockSpec(memory_space=pl.ANY)


def dot(a, b):
    return jnp.dot(a, b, preferred_element_type=F32)


def dot_nt(a, b):
    return lax.dot_general(a, b, (((1,), (1,)), ((), ())), preferred_element_type=F32)


def square_iota(n):
    return (
        lax.broadcasted_iota(jnp.int32, (n, n), 0),
        lax.broadcasted_iota(jnp.int32, (n, n), 1),
    )


def pack_kernel(
    atoms_ref, block_hbm, fit_ref, out_ref, table_ref, lines_ref,
    fits_ref, block_ref, flat_ref, sems, table_sem, block_sem,
):
    held = fit_ref.shape[0]
    half = fit_ref.shape[2] // 2
    row, col = square_iota(half)
    place = lax.broadcasted_iota(jnp.int32, (EXTRA, half), 0)
    fetches = [
        pltpu.make_async_copy(fit_ref.at[atom], fits_ref.at[atom], sems.at[atom])
        for atom in range(held)
    ]
    block = pltpu.make_async_copy(block_hbm, block_ref, block_sem)
    block.start()
    for fetch in fetches:
        fetch.start()
    table = pltpu.make_async_copy(atoms_ref, table_ref, table_sem)
    table.start()
    block.wait()
    row_count, column_count, chunks, lanes = lines_ref.shape
    for i in range(row_count):
        for q in range(chunks):
            flat_ref[i, q] = block_ref[i, :, q * lanes : (q + 1) * lanes].astype(F32)
    for i in range(row_count):
        for j in range(column_count):
            lines_ref[i, j] = flat_ref[i, :, j, :].astype(BF16)
    for atom in range(held):
        fetches[atom].wait()
        fit = fits_ref[atom]
        metric = lax.dot_general(fit, fit, (((0,), (0,)), ((), ())), preferred_element_type=F32)
        first, second = metric[:half, :half], metric[half:, half:]
        out_ref[atom, :half] = metric[:half, half:].astype(BF16)
        out_ref[atom, half : 2 * half] = jnp.where(row <= col, first, second).astype(BF16)
        lines = [jnp.sum(jnp.where(row == col, m, 0.0), axis=0, keepdims=True) for m in (first, second)]
        high = [line.astype(BF16).astype(F32) for line in lines]
        extra = jnp.where(
            place == 0,
            high[1],
            jnp.where(
                place == 1,
                lines[0] - high[0],
                jnp.where(place == 2, lines[1] - high[1], 0.0),
            ),
        )
        out_ref[atom, 2 * half :] = extra.astype(BF16)
    table.wait()


def unpack(packed, metric_ref):
    half = packed.shape[1]
    row, col = square_iota(half)
    corner = packed[:half]
    both = packed[half : 2 * half].astype(F32)
    extra = packed[2 * half :].astype(F32)
    turned = both.T
    metric_ref[:half, :half] = jnp.where(row <= col, both, turned).astype(BF16)
    metric_ref[:half, half:] = corner
    metric_ref[half:, :half] = corner.astype(F32).T.astype(BF16)
    metric_ref[half:, half:] = jnp.where(
        row > col, both, jnp.where(row == col, extra[0:1], turned)
    ).astype(BF16)
    return jnp.concatenate([extra[1:2], extra[2:3]], axis=1)


def ring_order(units):
    return [0] + list(range(1, units, 2)) + list(range(units - units % 2 - (0 if units % 2 else 2), 0, -2))


def ring_place(unit, units):
    return jnp.where(unit % 2 == 1, (unit + 1) // 2, (units - unit // 2) % units)


def pick_place(atom, row_place, col_place, cores, units, held):
    label = jnp.clip(atom - row_place * (units * cores * held), 0, units * cores * held - 1)
    owner, slot = label // held, label % held
    turn = (ring_place(col_place // cores, units) - ring_place(owner // cores, units) + units) % units
    side = (col_place % cores - owner % cores + cores) % cores
    return (turn * cores + side) * held + slot


def select_kernel(cores, units, pieces, atoms_ref, *refs):
    count = units * cores
    buffers, outs, all_ref = refs[:count], refs[count:-1], refs[-1]
    held = buffers[0].shape[0]
    row_place, col_place = lax.axis_index("row"), lax.axis_index("col")
    domain = atoms_ref.shape[0]
    columns = sum(pieces) // domain
    for index, buffer in enumerate(buffers):
        all_ref[index * held : (index + 1) * held] = buffer[...]
    targets = [(out, n) for out in outs for n in range(out.shape[0])]
    for index, (out, n) in enumerate(targets):
        atom = atoms_ref[index % domain, col_place * columns + index // domain]
        place = pick_place(atom, row_place, col_place, cores, units, held)
        out[n] = all_ref[place]


def pass_kernel(block_ref, *refs):
    refs[-1][...] = block_ref[...]


def neighbour_place(place, turn):
    return jnp.where(turn == 0, 0, jnp.where((place + turn) == jnp.bitwise_xor(place, 1), 1, 2))


def couple_kernel(partner_hbm, value_hbm, occupied_hbm, virtual_hbm, coef_hbm, inter_hbm, *refs):
    blocks = refs[:5]
    base_ref, row_turned_ref, turned_ref, coef_ref = refs[5:9]
    flat_ref, wide_ref, mats_ref, inters_ref, own_ref, inter_ref = refs[9:15]
    partner_ref, value_ref, occupied_ref, virtual_ref, sems, inter_sems, own_sems, coef_sems = refs[15:]
    row_count, column_count, terms, size = inter_ref.shape
    npno = base_ref.shape[2]
    lanes = 2 * npno
    chunks = size // lanes
    domain = coef_ref.shape[2]
    partners = terms // 2
    row_place, col_place = lax.axis_index("row"), lax.axis_index("col")
    first_row = row_place * row_count
    first_col = col_place * column_count
    fetches = [
        pltpu.make_async_copy(source, target, sems.at[n])
        for n, (source, target) in enumerate(
            [
                (partner_hbm, partner_ref),
                (value_hbm, value_ref),
                (occupied_hbm, occupied_ref),
                (virtual_hbm, virtual_ref),
            ]
        )
    ]

    def fetch_inter(i):
        return pltpu.make_async_copy(inter_hbm.at[i], inter_ref.at[i], inter_sems.at[i])

    def fetch_own(i):
        return pltpu.make_async_copy(
            coef_hbm.at[i, :, pl.ds(0, domain)], own_ref.at[i], own_sems.at[i]
        )

    def fetch_coef(i):
        return pltpu.make_async_copy(
            coef_hbm.at[i, :, pl.ds(domain, domain)], coef_ref.at[i], coef_sems.at[i]
        )

    for fetch in fetches:
        fetch.start()
    for i in range(row_count):
        fetch_inter(i).start()
    for i in range(row_count):
        fetch_own(i).start()
        fetch_coef(i).start()

    def square(lines):
        wide_ref[pl.ds(0, chunks, 2), :] = lines
        wide_ref[pl.ds(1, chunks, 2), :] = pltpu.roll(lines, npno, 1)
        return wide_ref[:, :npno]

    for index, block in enumerate(blocks):

        def one_block(i, carry, index=index, block=block):
            for j in range(column_count):
                mats_ref[index * row_count + i, j] = square(block[i, j].astype(F32)).astype(BF16)
            return carry

        lax.fori_loop(0, row_count, one_block, 0)
    for fetch in fetches:
        fetch.wait()

    def one_row(i, carry):
        fetch_inter(i).wait()
        fetch_own(i).wait()
        fetch_coef(i).wait()
        for j in range(column_count):
            for q in range(chunks):
                flat_ref[q] = inter_ref[i, j, :, q * lanes : (q + 1) * lanes].astype(F32)
            turned = []
            for n in range(terms):
                inter = square(flat_ref[:, n, :])
                inters_ref[n] = inter.astype(BF16)
                turned.append(inter.T.astype(BF16))
            total = jnp.zeros((npno, npno), F32)
            for n in range(terms):
                if n < partners:
                    away = partner_ref[n, first_row + i] - first_row + row_count
                    turn = away // row_count - 1
                    index = neighbour_place(row_place, turn) * row_count + away % row_count
                    weight = value_ref[n, first_row + i]
                    partner = mats_ref[index, j]
                else:
                    away = partner_ref[n - partners, first_col + j] - first_col + column_count
                    turn = away // column_count - 1
                    index = neighbour_place(col_place, turn)
                    index = jnp.where(index == 0, 0, index + 2) * row_count + i
                    weight = value_ref[n - partners, first_col + j]
                    partner = mats_ref[index, away % column_count]
                half = dot(inters_ref[n], partner).astype(BF16)
                total = total + weight * dot(half, turned[n])
            levels = jnp.broadcast_to(virtual_ref[i, pl.ds(j, 1)], (npno, npno))
            shift = levels + levels.T - occupied_ref[first_row + i] - occupied_ref[first_col + j]
            base_ref[i, j] = shift * mats_ref[i, j].astype(F32) - total
            for s in range(domain):
                row_turned_ref[i, s, j * npno : (j + 1) * npno] = own_ref[i, j, s].T[:npno]
                turned_ref[j, s, pl.ds(pl.multiple_of(i * npno, npno), npno)] = coef_ref[i, j, s].T[:npno]
        return carry

    lax.fori_loop(0, row_count, one_row, 0)


def row_kernel(cores, units, held, scale, atoms_ref, coef_hbm, turned_ref, base_ref, all_ref, *refs):
    out_ref, coef_ref, metric_ref, coef_sems = refs
    row_count, column_count, domain = coef_ref.shape[:3]
    npno = base_ref.shape[2]
    row_place, col_place = lax.axis_index("row"), lax.axis_index("col")

    def fetch(i):
        return pltpu.make_async_copy(
            coef_hbm.at[i, :, pl.ds(0, domain)], coef_ref.at[i], coef_sems.at[i]
        )

    for i in range(row_count):
        fetch(i).start()

    def one_row(i, carry):
        lows = []
        for s in range(domain):
            atom = atoms_ref[s, row_place * row_count + i]
            place = pick_place(atom, row_place, col_place, cores, units, held)
            lows.append(unpack(all_ref[place], metric_ref.at[s]))
        products = []
        for s in range(domain):
            left = turned_ref[i, s]
            product = dot(left, metric_ref[s]) + left.astype(F32) * lows[s]
            products.append(product.astype(BF16))
        fetch(i).wait()
        for j in range(column_count):
            total = dot(products[0][j * npno : (j + 1) * npno], coef_ref[i, j, 0])
            for s in range(1, domain):
                total = total + dot(products[s][j * npno : (j + 1) * npno], coef_ref[i, j, s])
            out_ref[i, j] = base_ref[i, j] + total[:, npno:] * scale
        return carry

    lax.fori_loop(0, row_count, one_row, 0)


def rows_away(column_count, row_count):
    source = lax.axis_index("col") * column_count // row_count
    return jnp.bitwise_xor(lax.axis_index("row"), source)


def merge_into(away, takers, kept, got, target):
    taken = functools.reduce(jnp.logical_or, [away == taker for taker in takers])

    @pl.when(taken)
    def _():
        target[...] = got[...]

    @pl.when(jnp.logical_not(taken))
    def _():
        target[...] = kept[...]


def merge_kernel(takers, column_count, row_count, *refs):
    count = len(takers)
    away = rows_away(column_count, row_count)
    for p in range(count):
        merge_into(away, takers[p], refs[p], refs[count + p], refs[2 * count + 1 + p])


def column_kernel(takers, scale, kept_hbm, coef_ref, turned_ref, base_ref, *refs):
    count = len(takers)
    out_ref, packed_ref, metric_ref, wide_ref, flat_ref, kept_ref, kept_sem = refs[2 * count :]
    row_count, column_count, domain = coef_ref.shape[:3]
    npno = base_ref.shape[2]
    lanes = 2 * npno
    kept_copy = pltpu.make_async_copy(kept_hbm, kept_ref, kept_sem)
    kept_copy.start()
    away = rows_away(column_count, row_count)
    start = 0
    for p in range(count):
        size = refs[p].shape[0]
        merge_into(away, takers[p], refs[p], refs[count + p], packed_ref.at[pl.ds(start, size)])
        start += size
    slots = column_count * domain
    lows = [unpack(packed_ref[index], metric_ref.at[index]) for index in range(slots)]
    products = []
    for index in range(slots):
        left = turned_ref[index // domain, index % domain]
        product = dot(left, metric_ref[index]) + left.astype(F32) * lows[index]
        products.append(product.astype(BF16))
    kept_copy.wait()
    row, col = square_iota(npno)
    lane = lax.broadcasted_iota(jnp.int32, (npno // 2, lanes), 1)
    for j in range(column_count):
        for i in range(row_count):
            total = None
            for s in range(domain):
                part = dot(products[j * domain + s][i * npno : (i + 1) * npno], coef_ref[i, j, s])
                total = part if total is None else total + part
            result = base_ref[i, j] + total[:, npno:] * scale
            kept = kept_ref[j, i]
            result = jnp.where((row < kept) & (col < kept), result, 0.0)
            wide_ref[i, j, :, :npno] = result
            even = wide_ref[i, j, pl.ds(0, npno // 2, 2), :]
            odd = wide_ref[i, j, pl.ds(1, npno // 2, 2), :]
            flat_ref[i, j] = jnp.where(lane < npno, even, pltpu.roll(odd, npno, 1))
    for i in range(row_count):
        for q in range(npno // 2):
            out_ref[i, :, q * lanes : (q + 1) * lanes] = flat_ref[i, :, q, :]


def call(kernel, out_shape, in_specs, out_specs, scratch, name, flops, moved):
    return pl.pallas_call(
        kernel,
        out_shape=out_shape,
        in_specs=in_specs,
        out_specs=out_specs,
        scratch_shapes=scratch,
        compiler_params=pltpu.CompilerParams(vmem_limit_bytes=48 * 2**20),
        cost_estimate=pl.CostEstimate(flops=flops, bytes_accessed=moved, transcendentals=0),
        name=name,
    )


def swapped(block, axis, first):
    size = lax.axis_size(axis)
    pairs = [(n, n + 1) for n in range(first, size - 1, 2)]
    return lax.ppermute(block, axis, pairs + [(b, a) for a, b in pairs])


def gather_metrics(packed, cores, units, first):
    order = ring_order(units)
    forward = [
        (order[n] * cores + k, order[(n + 1) % units] * cores + k)
        for n in range(units)
        for k in range(cores)
    ]
    backward = [(b, a) for a, b in forward]
    turns = [packed] + [None] * (units - 1)
    up = down = packed
    for step in range(1, units // 2 + 1):
        if step == 2:
            up = call(
                pass_kernel,
                jax.ShapeDtypeStruct(up.shape, up.dtype),
                [VMEM] + [ANY] * len(first),
                VMEM,
                [],
                "after_neighbours",
                0,
                0,
            )(up, *first)
        up = lax.ppermute(up, "col", forward)
        turns[step] = up
        if units - step > units // 2:
            down = lax.ppermute(down, "col", backward)
            turns[units - step] = down
    buffers = []
    for turn in turns:
        buffers.append(turn)
        for side in range(1, cores):
            swap = [
                (u * cores + k, u * cores + (k + side) % cores)
                for u in range(units)
                for k in range(cores)
            ]
            buffers.append(lax.ppermute(turn, "col", swap))
    return buffers


def spread(pieces, sources, column_count, row_count, first):
    rows, columns = lax.axis_size("row"), len(sources)
    bits = len(pieces)
    reached = [[0] for _ in pieces]
    for step in range(bits):
        got, takers = [], []
        for p in range(bits):
            bit = 1 << ((p + step) % bits)
            pairs = [
                ((sources[c] ^ away) * columns + c, (sources[c] ^ away ^ bit) * columns + c)
                for c in range(columns)
                for away in reached[p]
            ]
            got.append(lax.ppermute(pieces[p], ("row", "col"), pairs))
            takers.append([away ^ bit for away in reached[p]])
            reached[p] = reached[p] + takers[p]
        if step < bits - 1:
            pieces = call(
                functools.partial(merge_kernel, takers, column_count, row_count),
                tuple(jax.ShapeDtypeStruct(piece.shape, piece.dtype) for piece in pieces),
                [VMEM] * (2 * bits) + [ANY],
                (VMEM,) * bits,
                [],
                "merge",
                0,
                0,
            )(*pieces, *got, first)
    return list(pieces) + got, takers


def on_device(
    fitting,
    coefficients,
    amplitudes,
    intersections,
    virtual_energy,
    occupied_energy,
    kept_count,
    orbital_atoms,
    fock_partner,
    fock_value,
):
    row_count, column_count = amplitudes.shape[:2]
    held, aux, pao = fitting.shape
    domain = orbital_atoms.shape[1]
    npno = virtual_energy.shape[2]
    terms = intersections.shape[2]
    rows, columns = lax.axis_size("row"), lax.axis_size("col")
    cores = row_count // column_count
    units = columns // cores
    scale = (2 * domain * aux) ** (-0.5)
    depth = pao + EXTRA
    half = pao // 2

    chunks = npno // 2
    lanes = 2 * npno
    atoms_table, fit, own_block, partner, value, occupied, virtual, coefs, inter, kept = [
        pltpu.with_memory_space_constraint(array, pltpu.HBM)
        for array in (
            orbital_atoms.T,
            fitting,
            amplitudes,
            fock_partner.T,
            fock_value.T,
            occupied_energy,
            virtual_energy,
            coefficients,
            intersections,
            kept_count.T,
        )
    ]
    packed, table, lines = call(
        pack_kernel,
        (
            jax.ShapeDtypeStruct((held, depth, half), BF16),
            jax.ShapeDtypeStruct(atoms_table.shape, jnp.int32),
            jax.ShapeDtypeStruct((row_count, column_count, chunks, lanes), BF16),
        ),
        [HBM] * 3,
        (VMEM,) * 3,
        [
            pltpu.VMEM(fitting.shape, BF16),
            pltpu.VMEM(amplitudes.shape, BF16),
            pltpu.VMEM((row_count, chunks, column_count, lanes), F32),
            pltpu.SemaphoreType.DMA((held,)),
            pltpu.SemaphoreType.DMA(()),
            pltpu.SemaphoreType.DMA(()),
        ],
        "pack_metric",
        2 * held * aux * pao * pao,
        fitting.size * 2,
    )(atoms_table, own_block, fit)
    halos = [swapped(lines, axis, first) for axis in ("row", "col") for first in (0, 1)]
    buffers = gather_metrics(packed, cores, units, halos)
    blocks = [lines] + halos
    shape = (row_count, column_count, domain, pao, lanes)
    base, row_turned, turned, column_coefficients = call(
        couple_kernel,
        (
            jax.ShapeDtypeStruct((row_count, column_count, npno, npno), F32),
            jax.ShapeDtypeStruct((row_count, domain, column_count * npno, pao), BF16),
            jax.ShapeDtypeStruct((column_count, domain, row_count * npno, pao), BF16),
            jax.ShapeDtypeStruct(shape, BF16),
        ),
        [HBM] * 6 + [VMEM] * len(blocks),
        (VMEM,) * 4,
        [
            pltpu.VMEM((chunks, terms, lanes), F32),
            pltpu.VMEM((npno, lanes), F32),
            pltpu.VMEM((len(blocks) * row_count, column_count, npno, npno), BF16),
            pltpu.VMEM((terms, npno, npno), BF16),
            pltpu.VMEM(shape, BF16),
            pltpu.VMEM(intersections.shape, BF16),
            pltpu.SMEM(fock_partner.shape[::-1], jnp.int32),
            pltpu.SMEM(fock_value.shape[::-1], F32),
            pltpu.SMEM(occupied_energy.shape, F32),
            pltpu.VMEM(virtual_energy.shape, F32),
            pltpu.SemaphoreType.DMA((4,)),
            pltpu.SemaphoreType.DMA((row_count,)),
            pltpu.SemaphoreType.DMA((row_count,)),
            pltpu.SemaphoreType.DMA((row_count,)),
        ],
        "couple",
        4 * row_count * column_count * terms * npno**3,
        intersections.size * 4 + coefficients.size,
    )(partner, value, occupied, virtual, coefs, inter, *blocks)

    bits = rows.bit_length() - 1
    assert rows == 1 << bits
    wanted = column_count * domain
    sizes = [wanted * (p + 1) // bits - wanted * p // bits for p in range(bits)]
    atoms = len(buffers) * held
    *pieces, metrics = call(
        functools.partial(select_kernel, cores, units, sizes),
        tuple(jax.ShapeDtypeStruct((n, depth, half), BF16) for n in sizes + [atoms]),
        [SMEM] + [VMEM] * len(buffers),
        (VMEM,) * (bits + 1),
        [],
        "select_column_atoms",
        0,
        (wanted + 2 * atoms) * depth * half * 4,
    )(table, *buffers)
    sources = [c * column_count // row_count for c in range(columns)]
    pieces, takers = spread(pieces, sources, column_count, row_count, base)

    base = call(
        functools.partial(row_kernel, cores, units, held, scale),
        jax.ShapeDtypeStruct(base.shape, F32),
        [SMEM, HBM] + [VMEM] * 3,
        VMEM,
        [
            pltpu.VMEM(shape, BF16),
            pltpu.VMEM((domain, pao, pao), BF16),
            pltpu.SemaphoreType.DMA((row_count,)),
        ],
        "row_exchange",
        2 * row_count * column_count * domain * pao * npno * (pao + npno),
        coefficients.size,
    )(table, coefs, row_turned, base, metrics)

    return call(
        functools.partial(column_kernel, takers, scale),
        jax.ShapeDtypeStruct(amplitudes.shape, F32),
        [HBM] + [VMEM] * (3 + len(pieces)),
        VMEM,
        [
            pltpu.VMEM((wanted, depth, half), BF16),
            pltpu.VMEM((wanted, pao, pao), BF16),
            pltpu.VMEM((row_count, column_count, npno, lanes), F32),
            pltpu.VMEM((row_count, column_count, chunks, lanes), F32),
            pltpu.SMEM(kept_count.shape[::-1], jnp.int32),
            pltpu.SemaphoreType.DMA(()),
        ],
        "column_exchange",
        2 * row_count * column_count * domain * pao * npno * (pao + npno),
        coefficients.size,
    )(kept, column_coefficients, turned, base, *pieces)


def solution(mesh):
    placed = (
        P(("row", "col"), None, None),
        P("row", "col", None, None, None),
        P("row", "col", None),
        P("row", "col", None, None),
        P("row", "col", None),
        P(),
        P("row", "col"),
        P(),
        P(),
        P(),
    )
    return jax.shard_map(
        on_device, mesh=mesh, in_specs=placed, out_specs=P("row", "col", None), check_vma=False
    )
```

```python
import functools

import jax
import jax.numpy as jnp
from jax import lax
from jax.experimental import pallas as pl
from jax.experimental.pallas import tpu as pltpu
from jax.sharding import PartitionSpec as P

F32 = jnp.float32
BF16 = jnp.bfloat16
EXTRA = 16
VMEM = pl.BlockSpec(memory_space=pltpu.VMEM)
SMEM = pl.BlockSpec(memory_space=pltpu.SMEM)
HBM = pl.BlockSpec(memory_space=pltpu.HBM)
ANY = pl.BlockSpec(memory_space=pl.ANY)


def dot(a, b):
    return jnp.dot(a, b, preferred_element_type=F32)


def dot_nt(a, b):
    return lax.dot_general(a, b, (((1,), (1,)), ((), ())), preferred_element_type=F32)


def square_iota(n):
    return (
        lax.broadcasted_iota(jnp.int32, (n, n), 0),
        lax.broadcasted_iota(jnp.int32, (n, n), 1),
    )


def pack_kernel(
    atoms_ref, block_hbm, fit_ref, out_ref, table_ref, lines_ref,
    fits_ref, block_ref, flat_ref, sems, table_sem, block_sem,
):
    held = fit_ref.shape[0]
    half = fit_ref.shape[2] // 2
    row, col = square_iota(half)
    place = lax.broadcasted_iota(jnp.int32, (EXTRA, half), 0)
    fetches = [
        pltpu.make_async_copy(fit_ref.at[atom], fits_ref.at[atom], sems.at[atom])
        for atom in range(held)
    ]
    block = pltpu.make_async_copy(block_hbm, block_ref, block_sem)
    block.start()
    for fetch in fetches:
        fetch.start()
    table = pltpu.make_async_copy(atoms_ref, table_ref, table_sem)
    table.start()
    block.wait()
    row_count, column_count, chunks, lanes = lines_ref.shape
    for i in range(row_count):
        for q in range(chunks):
            flat_ref[i, q] = block_ref[i, :, q * lanes : (q + 1) * lanes].astype(F32)
    for i in range(row_count):
        for j in range(column_count):
            lines_ref[i, j] = flat_ref[i, :, j, :].astype(BF16)
    for atom in range(held):
        fetches[atom].wait()
        fit = fits_ref[atom]
        metric = lax.dot_general(fit, fit, (((0,), (0,)), ((), ())), preferred_element_type=F32)
        first, second = metric[:half, :half], metric[half:, half:]
        out_ref[atom, :half] = metric[:half, half:].astype(BF16)
        out_ref[atom, half : 2 * half] = jnp.where(row <= col, first, second).astype(BF16)
        lines = [jnp.sum(jnp.where(row == col, m, 0.0), axis=0, keepdims=True) for m in (first, second)]
        high = [line.astype(BF16).astype(F32) for line in lines]
        extra = jnp.where(
            place == 0,
            high[1],
            jnp.where(
                place == 1,
                lines[0] - high[0],
                jnp.where(place == 2, lines[1] - high[1], 0.0),
            ),
        )
        out_ref[atom, 2 * half :] = extra.astype(BF16)
    table.wait()


def unpack(packed, metric_ref):
    half = packed.shape[1]
    row, col = square_iota(half)
    corner = packed[:half]
    both = packed[half : 2 * half].astype(F32)
    extra = packed[2 * half :].astype(F32)
    turned = both.T
    metric_ref[:half, :half] = jnp.where(row <= col, both, turned).astype(BF16)
    metric_ref[:half, half:] = corner
    metric_ref[half:, :half] = corner.astype(F32).T.astype(BF16)
    metric_ref[half:, half:] = jnp.where(
        row > col, both, jnp.where(row == col, extra[0:1], turned)
    ).astype(BF16)
    return jnp.concatenate([extra[1:2], extra[2:3]], axis=1)


def ring_order(units):
    return [0] + list(range(1, units, 2)) + list(range(units - units % 2 - (0 if units % 2 else 2), 0, -2))


def ring_place(unit, units):
    return jnp.where(unit % 2 == 1, (unit + 1) // 2, (units - unit // 2) % units)


def pick_place(atom, row_place, col_place, cores, units, held):
    label = jnp.clip(atom - row_place * (units * cores * held), 0, units * cores * held - 1)
    owner, slot = label // held, label % held
    turn = (ring_place(col_place // cores, units) - ring_place(owner // cores, units) + units) % units
    side = (col_place % cores - owner % cores + cores) % cores
    return (turn * cores + side) * held + slot


def select_kernel(cores, units, atoms_ref, *refs):
    count = units * cores
    buffers, (piece_ref, all_ref) = refs[:count], refs[-2:]
    held = buffers[0].shape[0]
    row_place, col_place = lax.axis_index("row"), lax.axis_index("col")
    domain = atoms_ref.shape[0]
    wanted = piece_ref.shape[0]
    for index, buffer in enumerate(buffers):
        all_ref[index * held : (index + 1) * held] = buffer[...]
    for index in range(wanted):
        atom = atoms_ref[index % domain, col_place * (wanted // domain) + index // domain]
        place = pick_place(atom, row_place, col_place, cores, units, held)
        piece_ref[index] = all_ref[place]


def pass_kernel(block_ref, *refs):
    refs[-1][...] = block_ref[...]


def neighbour_place(place, turn):
    return jnp.where(turn == 0, 0, jnp.where((place + turn) == jnp.bitwise_xor(place, 1), 1, 2))


def couple_kernel(partner_hbm, value_hbm, occupied_hbm, virtual_hbm, coef_hbm, inter_hbm, *refs):
    blocks = refs[:5]
    base_ref, row_turned_ref, turned_ref, coef_ref = refs[5:9]
    flat_ref, wide_ref, mats_ref, inters_ref, own_ref, inter_ref = refs[9:15]
    partner_ref, value_ref, occupied_ref, virtual_ref, sems, inter_sems, own_sems, coef_sems = refs[15:]
    row_count, column_count, terms, size = inter_ref.shape
    npno = base_ref.shape[2]
    lanes = 2 * npno
    chunks = size // lanes
    domain = coef_ref.shape[2]
    partners = terms // 2
    row_place, col_place = lax.axis_index("row"), lax.axis_index("col")
    first_row = row_place * row_count
    first_col = col_place * column_count
    fetches = [
        pltpu.make_async_copy(source, target, sems.at[n])
        for n, (source, target) in enumerate(
            [
                (partner_hbm, partner_ref),
                (value_hbm, value_ref),
                (occupied_hbm, occupied_ref),
                (virtual_hbm, virtual_ref),
            ]
        )
    ]

    def fetch_inter(i):
        return pltpu.make_async_copy(inter_hbm.at[i], inter_ref.at[i], inter_sems.at[i])

    def fetch_own(i):
        return pltpu.make_async_copy(
            coef_hbm.at[i, :, pl.ds(0, domain)], own_ref.at[i], own_sems.at[i]
        )

    def fetch_coef(i):
        return pltpu.make_async_copy(
            coef_hbm.at[i, :, pl.ds(domain, domain)], coef_ref.at[i], coef_sems.at[i]
        )

    for fetch in fetches:
        fetch.start()
    for i in range(row_count):
        fetch_inter(i).start()
    for i in range(row_count):
        fetch_own(i).start()
        fetch_coef(i).start()

    def square(lines):
        wide_ref[pl.ds(0, chunks, 2), :] = lines
        wide_ref[pl.ds(1, chunks, 2), :] = pltpu.roll(lines, npno, 1)
        return wide_ref[:, :npno]

    for index, block in enumerate(blocks):

        def one_block(i, carry, index=index, block=block):
            for j in range(column_count):
                mats_ref[index * row_count + i, j] = square(block[i, j].astype(F32)).astype(BF16)
            return carry

        lax.fori_loop(0, row_count, one_block, 0)
    for fetch in fetches:
        fetch.wait()

    def one_row(i, carry):
        fetch_inter(i).wait()
        fetch_own(i).wait()
        fetch_coef(i).wait()
        for j in range(column_count):
            for q in range(chunks):
                flat_ref[q] = inter_ref[i, j, :, q * lanes : (q + 1) * lanes].astype(F32)
            turned = []
            for n in range(terms):
                inter = square(flat_ref[:, n, :])
                inters_ref[n] = inter.astype(BF16)
                turned.append(inter.T.astype(BF16))
            total = jnp.zeros((npno, npno), F32)
            for n in range(terms):
                if n < partners:
                    away = partner_ref[n, first_row + i] - first_row + row_count
                    turn = away // row_count - 1
                    index = neighbour_place(row_place, turn) * row_count + away % row_count
                    weight = value_ref[n, first_row + i]
                    partner = mats_ref[index, j]
                else:
                    away = partner_ref[n - partners, first_col + j] - first_col + column_count
                    turn = away // column_count - 1
                    index = neighbour_place(col_place, turn)
                    index = jnp.where(index == 0, 0, index + 2) * row_count + i
                    weight = value_ref[n - partners, first_col + j]
                    partner = mats_ref[index, away % column_count]
                half = dot(inters_ref[n], partner).astype(BF16)
                total = total + weight * dot(half, turned[n])
            levels = jnp.broadcast_to(virtual_ref[i, pl.ds(j, 1)], (npno, npno))
            shift = levels + levels.T - occupied_ref[first_row + i] - occupied_ref[first_col + j]
            base_ref[i, j] = shift * mats_ref[i, j].astype(F32) - total
            for s in range(domain):
                row_turned_ref[i, s, j * npno : (j + 1) * npno] = own_ref[i, j, s].T[:npno]
                turned_ref[j, s, pl.ds(pl.multiple_of(i * npno, npno), npno)] = coef_ref[i, j, s].T[:npno]
        return carry

    lax.fori_loop(0, row_count, one_row, 0)


def row_kernel(cores, units, held, scale, atoms_ref, coef_hbm, turned_ref, base_ref, all_ref, *refs):
    out_ref, coef_ref, metric_ref, coef_sems = refs
    row_count, column_count, domain = coef_ref.shape[:3]
    npno = base_ref.shape[2]
    row_place, col_place = lax.axis_index("row"), lax.axis_index("col")

    def fetch(i):
        return pltpu.make_async_copy(
            coef_hbm.at[i, :, pl.ds(0, domain)], coef_ref.at[i], coef_sems.at[i]
        )

    for i in range(row_count):
        fetch(i).start()

    def one_row(i, carry):
        lows = []
        for s in range(domain):
            atom = atoms_ref[s, row_place * row_count + i]
            place = pick_place(atom, row_place, col_place, cores, units, held)
            lows.append(unpack(all_ref[place], metric_ref.at[s]))
        products = []
        for s in range(domain):
            left = turned_ref[i, s]
            product = dot(left, metric_ref[s]) + left.astype(F32) * lows[s]
            products.append(product.astype(BF16))
        fetch(i).wait()
        for j in range(column_count):
            total = dot(products[0][j * npno : (j + 1) * npno], coef_ref[i, j, 0])
            for s in range(1, domain):
                total = total + dot(products[s][j * npno : (j + 1) * npno], coef_ref[i, j, s])
            out_ref[i, j] = base_ref[i, j] + total[:, npno:] * scale
        return carry

    lax.fori_loop(0, row_count, one_row, 0)


def merge_into(takers, column_count, row_count, kept, got, target):
    col_place = lax.axis_index("col")
    away = jnp.bitwise_xor(lax.axis_index("row"), col_place * column_count // row_count)
    turn = col_place % len(takers)
    taken = functools.reduce(
        jnp.logical_or,
        [(turn == n) & (away == taker) for n, these in enumerate(takers) for taker in these],
    )

    @pl.when(taken)
    def _():
        target[...] = got[...]

    @pl.when(jnp.logical_not(taken))
    def _():
        target[...] = kept[...]


def merge_kernel(takers, column_count, row_count, kept_ref, got_ref, _, out_ref):
    merge_into(takers, column_count, row_count, kept_ref, got_ref, out_ref)


def column_kernel(
    takers, scale, kept_hbm, coef_ref, turned_ref, base_ref, held_ref, got_ref,
    out_ref, packed_ref, metric_ref, wide_ref, flat_ref, kept_ref, kept_sem,
):
    row_count, column_count, domain = coef_ref.shape[:3]
    npno = base_ref.shape[2]
    lanes = 2 * npno
    kept_copy = pltpu.make_async_copy(kept_hbm, kept_ref, kept_sem)
    kept_copy.start()
    merge_into(takers, column_count, row_count, held_ref, got_ref, packed_ref)
    slots = column_count * domain
    lows = [unpack(packed_ref[index], metric_ref.at[index]) for index in range(slots)]
    products = []
    for index in range(slots):
        left = turned_ref[index // domain, index % domain]
        product = dot(left, metric_ref[index]) + left.astype(F32) * lows[index]
        products.append(product.astype(BF16))
    kept_copy.wait()
    row, col = square_iota(npno)
    lane = lax.broadcasted_iota(jnp.int32, (npno // 2, lanes), 1)
    for j in range(column_count):
        for i in range(row_count):
            total = None
            for s in range(domain):
                part = dot(products[j * domain + s][i * npno : (i + 1) * npno], coef_ref[i, j, s])
                total = part if total is None else total + part
            result = base_ref[i, j] + total[:, npno:] * scale
            kept = kept_ref[j, i]
            result = jnp.where((row < kept) & (col < kept), result, 0.0)
            wide_ref[i, j, :, :npno] = result
            even = wide_ref[i, j, pl.ds(0, npno // 2, 2), :]
            odd = wide_ref[i, j, pl.ds(1, npno // 2, 2), :]
            flat_ref[i, j] = jnp.where(lane < npno, even, pltpu.roll(odd, npno, 1))
    for i in range(row_count):
        for q in range(npno // 2):
            out_ref[i, :, q * lanes : (q + 1) * lanes] = flat_ref[i, :, q, :]


def call(kernel, out_shape, in_specs, out_specs, scratch, name, flops, moved):
    return pl.pallas_call(
        kernel,
        out_shape=out_shape,
        in_specs=in_specs,
        out_specs=out_specs,
        scratch_shapes=scratch,
        compiler_params=pltpu.CompilerParams(vmem_limit_bytes=48 * 2**20),
        cost_estimate=pl.CostEstimate(flops=flops, bytes_accessed=moved, transcendentals=0),
        name=name,
    )


def swapped(block, axis, first):
    size = lax.axis_size(axis)
    pairs = [(n, n + 1) for n in range(first, size - 1, 2)]
    return lax.ppermute(block, axis, pairs + [(b, a) for a, b in pairs])


def after(block, others):
    return call(
        pass_kernel,
        jax.ShapeDtypeStruct(block.shape, block.dtype),
        [VMEM] + [ANY] * len(others),
        VMEM,
        [],
        "after_others",
        0,
        0,
    )(block, *others)


def gather_metrics(packed, cores, units, first, second):
    order = ring_order(units)
    forward = [
        (order[n] * cores + k, order[(n + 1) % units] * cores + k)
        for n in range(units)
        for k in range(cores)
    ]
    backward = [(b, a) for a, b in forward]
    turns = [packed] + [None] * (units - 1)
    up = down = packed
    for step in range(1, units // 2 + 1):
        if step == 2:
            up = after(up, first)
        up = lax.ppermute(up, "col", forward)
        if step == 2:
            up = after(up, second)
        turns[step] = up
        if units - step > units // 2:
            down = lax.ppermute(down, "col", backward)
            turns[units - step] = down
    buffers = []
    for turn in turns:
        buffers.append(turn)
        for side in range(1, cores):
            swap = [
                (u * cores + k, u * cores + (k + side) % cores)
                for u in range(units)
                for k in range(cores)
            ]
            buffers.append(lax.ppermute(turn, "col", swap))
    return buffers


def spread(piece, sources, column_count, row_count, first):
    rows, columns = lax.axis_size("row"), len(sources)
    bits = rows.bit_length() - 1
    assert rows == 1 << bits
    reached = [[0] for _ in range(bits)]
    for step in range(bits):
        pairs, takers = [], []
        for turn in range(bits):
            bit = 1 << ((turn + step) % bits)
            pairs += [
                ((sources[c] ^ away) * columns + c, (sources[c] ^ away ^ bit) * columns + c)
                for c in range(turn, columns, bits)
                for away in reached[turn]
            ]
            takers.append([away ^ bit for away in reached[turn]])
            reached[turn] = reached[turn] + takers[turn]
        got = lax.ppermute(piece, ("row", "col"), pairs)
        if step < bits - 1:
            piece = call(
                functools.partial(merge_kernel, takers, column_count, row_count),
                jax.ShapeDtypeStruct(piece.shape, piece.dtype),
                [VMEM, VMEM, ANY],
                VMEM,
                [],
                "merge",
                0,
                0,
            )(piece, got, first)
    return piece, got, takers


def on_device(
    fitting,
    coefficients,
    amplitudes,
    intersections,
    virtual_energy,
    occupied_energy,
    kept_count,
    orbital_atoms,
    fock_partner,
    fock_value,
):
    row_count, column_count = amplitudes.shape[:2]
    held, aux, pao = fitting.shape
    domain = orbital_atoms.shape[1]
    npno = virtual_energy.shape[2]
    terms = intersections.shape[2]
    columns = lax.axis_size("col")
    cores = row_count // column_count
    units = columns // cores
    scale = (2 * domain * aux) ** (-0.5)
    depth = pao + EXTRA
    half = pao // 2

    chunks = npno // 2
    lanes = 2 * npno
    atoms_table, fit, own_block, partner, value, occupied, virtual, coefs, inter, kept = [
        pltpu.with_memory_space_constraint(array, pltpu.HBM)
        for array in (
            orbital_atoms.T,
            fitting,
            amplitudes,
            fock_partner.T,
            fock_value.T,
            occupied_energy,
            virtual_energy,
            coefficients,
            intersections,
            kept_count.T,
        )
    ]
    packed, table, lines = call(
        pack_kernel,
        (
            jax.ShapeDtypeStruct((held, depth, half), BF16),
            jax.ShapeDtypeStruct(atoms_table.shape, jnp.int32),
            jax.ShapeDtypeStruct((row_count, column_count, chunks, lanes), BF16),
        ),
        [HBM] * 3,
        (VMEM,) * 3,
        [
            pltpu.VMEM(fitting.shape, BF16),
            pltpu.VMEM(amplitudes.shape, BF16),
            pltpu.VMEM((row_count, chunks, column_count, lanes), F32),
            pltpu.SemaphoreType.DMA((held,)),
            pltpu.SemaphoreType.DMA(()),
            pltpu.SemaphoreType.DMA(()),
        ],
        "pack_metric",
        2 * held * aux * pao * pao,
        fitting.size * 2,
    )(atoms_table, own_block, fit)
    halos = [swapped(lines, axis, first) for axis in ("row", "col") for first in (0, 1)]
    buffers = gather_metrics(packed, cores, units, halos[2:], halos[:2])
    blocks = [lines] + halos
    shape = (row_count, column_count, domain, pao, lanes)
    base, row_turned, turned, column_coefficients = call(
        couple_kernel,
        (
            jax.ShapeDtypeStruct((row_count, column_count, npno, npno), F32),
            jax.ShapeDtypeStruct((row_count, domain, column_count * npno, pao), BF16),
            jax.ShapeDtypeStruct((column_count, domain, row_count * npno, pao), BF16),
            jax.ShapeDtypeStruct(shape, BF16),
        ),
        [HBM] * 6 + [VMEM] * len(blocks),
        (VMEM,) * 4,
        [
            pltpu.VMEM((chunks, terms, lanes), F32),
            pltpu.VMEM((npno, lanes), F32),
            pltpu.VMEM((len(blocks) * row_count, column_count, npno, npno), BF16),
            pltpu.VMEM((terms, npno, npno), BF16),
            pltpu.VMEM(shape, BF16),
            pltpu.VMEM(intersections.shape, BF16),
            pltpu.SMEM(fock_partner.shape[::-1], jnp.int32),
            pltpu.SMEM(fock_value.shape[::-1], F32),
            pltpu.SMEM(occupied_energy.shape, F32),
            pltpu.VMEM(virtual_energy.shape, F32),
            pltpu.SemaphoreType.DMA((4,)),
            pltpu.SemaphoreType.DMA((row_count,)),
            pltpu.SemaphoreType.DMA((row_count,)),
            pltpu.SemaphoreType.DMA((row_count,)),
        ],
        "couple",
        4 * row_count * column_count * terms * npno**3,
        intersections.size * 4 + coefficients.size,
    )(partner, value, occupied, virtual, coefs, inter, *blocks)

    wanted = column_count * domain
    atoms = len(buffers) * held
    piece, metrics = call(
        functools.partial(select_kernel, cores, units),
        tuple(jax.ShapeDtypeStruct((n, depth, half), BF16) for n in (wanted, atoms)),
        [SMEM] + [VMEM] * len(buffers),
        (VMEM,) * 2,
        [],
        "select_column_atoms",
        0,
        (wanted + 2 * atoms) * depth * half * 4,
    )(table, *buffers)
    sources = [c * column_count // row_count for c in range(columns)]
    piece, got, takers = spread(piece, sources, column_count, row_count, base)

    base = call(
        functools.partial(row_kernel, cores, units, held, scale),
        jax.ShapeDtypeStruct(base.shape, F32),
        [SMEM, HBM] + [VMEM] * 3,
        VMEM,
        [
            pltpu.VMEM(shape, BF16),
            pltpu.VMEM((domain, pao, pao), BF16),
            pltpu.SemaphoreType.DMA((row_count,)),
        ],
        "row_exchange",
        2 * row_count * column_count * domain * pao * npno * (pao + npno),
        coefficients.size,
    )(table, coefs, row_turned, base, metrics)

    return call(
        functools.partial(column_kernel, takers, scale),
        jax.ShapeDtypeStruct(amplitudes.shape, F32),
        [HBM] + [VMEM] * 5,
        VMEM,
        [
            pltpu.VMEM((wanted, depth, half), BF16),
            pltpu.VMEM((wanted, pao, pao), BF16),
            pltpu.VMEM((row_count, column_count, npno, lanes), F32),
            pltpu.VMEM((row_count, column_count, chunks, lanes), F32),
            pltpu.SMEM(kept_count.shape[::-1], jnp.int32),
            pltpu.SemaphoreType.DMA(()),
        ],
        "column_exchange",
        2 * row_count * column_count * domain * pao * npno * (pao + npno),
        coefficients.size,
    )(kept, column_coefficients, turned, base, piece, got)


def solution(mesh):
    placed = (
        P(("row", "col"), None, None),
        P("row", "col", None, None, None),
        P("row", "col", None),
        P("row", "col", None, None),
        P("row", "col", None),
        P(),
        P("row", "col"),
        P(),
        P(),
        P(),
    )
    return jax.shard_map(
        on_device, mesh=mesh, in_specs=placed, out_specs=P("row", "col", None), check_vma=False
    )
```

```python
import functools

import jax
import jax.numpy as jnp
from jax import lax
from jax.experimental import pallas as pl
from jax.experimental.pallas import tpu as pltpu
from jax.sharding import PartitionSpec as P

F32 = jnp.float32
BF16 = jnp.bfloat16
EXTRA = 16
VMEM = pl.BlockSpec(memory_space=pltpu.VMEM)
SMEM = pl.BlockSpec(memory_space=pltpu.SMEM)
HBM = pl.BlockSpec(memory_space=pltpu.HBM)
ANY = pl.BlockSpec(memory_space=pl.ANY)


def dot(a, b):
    return jnp.dot(a, b, preferred_element_type=F32)


def dot_nt(a, b):
    return lax.dot_general(a, b, (((1,), (1,)), ((), ())), preferred_element_type=F32)


def square_iota(n):
    return (
        lax.broadcasted_iota(jnp.int32, (n, n), 0),
        lax.broadcasted_iota(jnp.int32, (n, n), 1),
    )


def pack_kernel(
    atoms_ref, block_hbm, fit_ref, out_ref, table_ref, lines_ref,
    fits_ref, block_ref, flat_ref, sems, table_sem, block_sem,
):
    held = fit_ref.shape[0]
    half = fit_ref.shape[2] // 2
    row, col = square_iota(half)
    place = lax.broadcasted_iota(jnp.int32, (EXTRA, half), 0)
    fetches = [
        pltpu.make_async_copy(fit_ref.at[atom], fits_ref.at[atom], sems.at[atom])
        for atom in range(held)
    ]
    block = pltpu.make_async_copy(block_hbm, block_ref, block_sem)
    block.start()
    for fetch in fetches:
        fetch.start()
    table = pltpu.make_async_copy(atoms_ref, table_ref, table_sem)
    table.start()
    block.wait()
    row_count, column_count, chunks, lanes = lines_ref.shape
    for i in range(row_count):
        for q in range(chunks):
            flat_ref[i, q] = block_ref[i, :, q * lanes : (q + 1) * lanes].astype(F32)
    for i in range(row_count):
        for j in range(column_count):
            lines_ref[i, j] = flat_ref[i, :, j, :].astype(BF16)
    for atom in range(held):
        fetches[atom].wait()
        fit = fits_ref[atom]
        metric = lax.dot_general(fit, fit, (((0,), (0,)), ((), ())), preferred_element_type=F32)
        first, second = metric[:half, :half], metric[half:, half:]
        out_ref[atom, :half] = metric[:half, half:].astype(BF16)
        out_ref[atom, half : 2 * half] = jnp.where(row <= col, first, second).astype(BF16)
        lines = [jnp.sum(jnp.where(row == col, m, 0.0), axis=0, keepdims=True) for m in (first, second)]
        high = [line.astype(BF16).astype(F32) for line in lines]
        extra = jnp.where(
            place == 0,
            high[1],
            jnp.where(
                place == 1,
                lines[0] - high[0],
                jnp.where(place == 2, lines[1] - high[1], 0.0),
            ),
        )
        out_ref[atom, 2 * half :] = extra.astype(BF16)
    table.wait()


def unpack(packed, metric_ref):
    half = packed.shape[1]
    row, col = square_iota(half)
    corner = packed[:half]
    both = packed[half : 2 * half].astype(F32)
    extra = packed[2 * half :].astype(F32)
    turned = both.T
    metric_ref[:half, :half] = jnp.where(row <= col, both, turned).astype(BF16)
    metric_ref[:half, half:] = corner
    metric_ref[half:, :half] = corner.astype(F32).T.astype(BF16)
    metric_ref[half:, half:] = jnp.where(
        row > col, both, jnp.where(row == col, extra[0:1], turned)
    ).astype(BF16)
    return jnp.concatenate([extra[1:2], extra[2:3]], axis=1)


def ring_order(units):
    return [0] + list(range(1, units, 2)) + list(range(units - units % 2 - (0 if units % 2 else 2), 0, -2))


def ring_place(unit, units):
    return jnp.where(unit % 2 == 1, (unit + 1) // 2, (units - unit // 2) % units)


def pick_place(atom, row_place, col_place, cores, units, held):
    label = jnp.clip(atom - row_place * (units * cores * held), 0, units * cores * held - 1)
    owner, slot = label // held, label % held
    turn = (ring_place(col_place // cores, units) - ring_place(owner // cores, units) + units) % units
    side = (col_place % cores - owner % cores + cores) % cores
    return (turn * cores + side) * held + slot


def select_kernel(cores, units, atoms_ref, *refs):
    count = units * cores
    buffers, (piece_ref, all_ref) = refs[:count], refs[-2:]
    held = buffers[0].shape[0]
    row_place, col_place = lax.axis_index("row"), lax.axis_index("col")
    domain = atoms_ref.shape[0]
    wanted = piece_ref.shape[0]
    for index, buffer in enumerate(buffers):
        all_ref[index * held : (index + 1) * held] = buffer[...]
    for index in range(wanted):
        atom = atoms_ref[index % domain, col_place * (wanted // domain) + index // domain]
        place = pick_place(atom, row_place, col_place, cores, units, held)
        piece_ref[index] = all_ref[place]


def pass_kernel(block_ref, *refs):
    refs[-1][...] = block_ref[...]


def neighbour_place(place, turn):
    return jnp.where(turn == 0, 0, jnp.where((place + turn) == jnp.bitwise_xor(place, 1), 1, 2))


def couple_kernel(partner_hbm, value_hbm, occupied_hbm, virtual_hbm, inter_hbm, *refs):
    exchange_ref, blocks = refs[0], refs[1:6]
    base_ref, flat_ref, wide_ref, mats_ref, inters_ref, inter_ref = refs[6:12]
    partner_ref, value_ref, occupied_ref, virtual_ref, sems, inter_sems = refs[12:]
    row_count, column_count, terms, size = inter_ref.shape
    npno = base_ref.shape[2]
    lanes = 2 * npno
    chunks = size // lanes
    partners = terms // 2
    row_place, col_place = lax.axis_index("row"), lax.axis_index("col")
    first_row = row_place * row_count
    first_col = col_place * column_count
    fetches = [
        pltpu.make_async_copy(source, target, sems.at[n])
        for n, (source, target) in enumerate(
            [
                (partner_hbm, partner_ref),
                (value_hbm, value_ref),
                (occupied_hbm, occupied_ref),
                (virtual_hbm, virtual_ref),
            ]
        )
    ]

    def fetch_inter(i):
        return pltpu.make_async_copy(inter_hbm.at[i], inter_ref.at[i], inter_sems.at[i])

    for fetch in fetches:
        fetch.start()
    for i in range(row_count):
        fetch_inter(i).start()
    def square(lines):
        wide_ref[pl.ds(0, chunks, 2), :] = lines
        wide_ref[pl.ds(1, chunks, 2), :] = pltpu.roll(lines, npno, 1)
        return wide_ref[:, :npno]

    for index, block in enumerate(blocks):

        def one_block(i, carry, index=index, block=block):
            for j in range(column_count):
                mats_ref[index * row_count + i, j] = square(block[i, j].astype(F32)).astype(BF16)
            return carry

        lax.fori_loop(0, row_count, one_block, 0)
    for fetch in fetches:
        fetch.wait()

    def one_row(i, carry):
        fetch_inter(i).wait()
        for j in range(column_count):
            for q in range(chunks):
                flat_ref[q] = inter_ref[i, j, :, q * lanes : (q + 1) * lanes].astype(F32)
            turned = []
            for n in range(terms):
                inter = square(flat_ref[:, n, :])
                inters_ref[n] = inter.astype(BF16)
                turned.append(inter.T.astype(BF16))
            total = jnp.zeros((npno, npno), F32)
            for n in range(terms):
                if n < partners:
                    away = partner_ref[n, first_row + i] - first_row + row_count
                    turn = away // row_count - 1
                    index = neighbour_place(row_place, turn) * row_count + away % row_count
                    weight = value_ref[n, first_row + i]
                    partner = mats_ref[index, j]
                else:
                    away = partner_ref[n - partners, first_col + j] - first_col + column_count
                    turn = away // column_count - 1
                    index = neighbour_place(col_place, turn)
                    index = jnp.where(index == 0, 0, index + 2) * row_count + i
                    weight = value_ref[n - partners, first_col + j]
                    partner = mats_ref[index, away % column_count]
                half = dot(inters_ref[n], partner).astype(BF16)
                total = total + weight * dot(half, turned[n])
            levels = jnp.broadcast_to(virtual_ref[i, pl.ds(j, 1)], (npno, npno))
            shift = levels + levels.T - occupied_ref[first_row + i] - occupied_ref[first_col + j]
            base_ref[i, j] = exchange_ref[i, j] + shift * mats_ref[i, j].astype(F32) - total
        return carry

    lax.fori_loop(0, row_count, one_row, 0)


def prepare_kernel(coef_hbm, own_ref, coef_ref, own_turned_ref, turned_ref, own_sems, coef_sems):
    row_count, column_count, domain, _, lanes = own_ref.shape
    npno = lanes // 2

    def fetch(i, first, target_ref, sems):
        return pltpu.make_async_copy(
            coef_hbm.at[i, :, pl.ds(first, domain)], target_ref.at[i], sems.at[i]
        )

    for i in range(row_count):
        fetch(i, 0, own_ref, own_sems).start()
        fetch(i, domain, coef_ref, coef_sems).start()
    for i in range(row_count):
        fetch(i, 0, own_ref, own_sems).wait()
        for j in range(column_count):
            for s in range(domain):
                own_turned_ref[i, s, j * npno : (j + 1) * npno] = own_ref[i, j, s].T[:npno]
        fetch(i, domain, coef_ref, coef_sems).wait()
        for j in range(column_count):
            for s in range(domain):
                turned_ref[j, s, i * npno : (i + 1) * npno] = coef_ref[i, j, s].T[:npno]


def row_kernel(cores, units, held, scale, atoms_ref, coef_ref, turned_ref, all_ref, out_ref, metric_ref):
    row_count, column_count, domain = coef_ref.shape[:3]
    npno = out_ref.shape[2]
    row_place, col_place = lax.axis_index("row"), lax.axis_index("col")

    def one_row(i, carry):
        lows = []
        for s in range(domain):
            atom = atoms_ref[s, row_place * row_count + i]
            place = pick_place(atom, row_place, col_place, cores, units, held)
            lows.append(unpack(all_ref[place], metric_ref.at[s]))
        products = []
        for s in range(domain):
            left = turned_ref[i, s]
            product = dot(left, metric_ref[s]) + left.astype(F32) * lows[s]
            products.append(product.astype(BF16))
        for j in range(column_count):
            total = dot(products[0][j * npno : (j + 1) * npno], coef_ref[i, j, 0])
            for s in range(1, domain):
                total = total + dot(products[s][j * npno : (j + 1) * npno], coef_ref[i, j, s])
            out_ref[i, j] = total[:, npno:] * scale
        return carry

    lax.fori_loop(0, row_count, one_row, 0)


def merge_into(takers, column_count, row_count, kept, got, target):
    col_place = lax.axis_index("col")
    away = jnp.bitwise_xor(lax.axis_index("row"), col_place * column_count // row_count)
    turn = col_place % len(takers)
    taken = functools.reduce(
        jnp.logical_or,
        [(turn == n) & (away == taker) for n, these in enumerate(takers) for taker in these],
    )

    @pl.when(taken)
    def _():
        target[...] = got[...]

    @pl.when(jnp.logical_not(taken))
    def _():
        target[...] = kept[...]


def merge_kernel(takers, column_count, row_count, kept_ref, got_ref, *refs):
    merge_into(takers, column_count, row_count, kept_ref, got_ref, refs[-1])


def column_kernel(
    takers, scale, kept_hbm, coef_ref, turned_ref, base_ref, held_ref, got_ref,
    out_ref, packed_ref, metric_ref, wide_ref, flat_ref, kept_ref, kept_sem,
):
    row_count, column_count, domain = coef_ref.shape[:3]
    npno = base_ref.shape[2]
    lanes = 2 * npno
    kept_copy = pltpu.make_async_copy(kept_hbm, kept_ref, kept_sem)
    kept_copy.start()
    merge_into(takers, column_count, row_count, held_ref, got_ref, packed_ref)
    slots = column_count * domain
    lows = [unpack(packed_ref[index], metric_ref.at[index]) for index in range(slots)]
    products = []
    for index in range(slots):
        left = turned_ref[index // domain, index % domain]
        product = dot(left, metric_ref[index]) + left.astype(F32) * lows[index]
        products.append(product.astype(BF16))
    kept_copy.wait()
    row, col = square_iota(npno)
    lane = lax.broadcasted_iota(jnp.int32, (npno // 2, lanes), 1)
    for j in range(column_count):
        for i in range(row_count):
            total = None
            for s in range(domain):
                part = dot(products[j * domain + s][i * npno : (i + 1) * npno], coef_ref[i, j, s])
                total = part if total is None else total + part
            result = base_ref[i, j] + total[:, npno:] * scale
            kept = kept_ref[j, i]
            result = jnp.where((row < kept) & (col < kept), result, 0.0)
            wide_ref[i, j, :, :npno] = result
            even = wide_ref[i, j, pl.ds(0, npno // 2, 2), :]
            odd = wide_ref[i, j, pl.ds(1, npno // 2, 2), :]
            flat_ref[i, j] = jnp.where(lane < npno, even, pltpu.roll(odd, npno, 1))
    for i in range(row_count):
        for q in range(npno // 2):
            out_ref[i, :, q * lanes : (q + 1) * lanes] = flat_ref[i, :, q, :]


def call(kernel, out_shape, in_specs, out_specs, scratch, name, flops, moved):
    return pl.pallas_call(
        kernel,
        out_shape=out_shape,
        in_specs=in_specs,
        out_specs=out_specs,
        scratch_shapes=scratch,
        compiler_params=pltpu.CompilerParams(vmem_limit_bytes=48 * 2**20),
        cost_estimate=pl.CostEstimate(flops=flops, bytes_accessed=moved, transcendentals=0),
        name=name,
    )


def partners_of(size, first):
    pairs = [(n, n + 1) for n in range(first, size - 1, 2)]
    alone = [(n, n) for n in range(size) if n < first or n >= first + 2 * len(pairs)]
    return pairs, pairs + [(b, a) for a, b in pairs] + alone


def neighbours(block, axis):
    size = lax.axis_size(axis)
    even = lax.ppermute(block, axis, partners_of(size, 0)[1])
    pairs, route = partners_of(size, 1)
    if size % 4 == 0 and axis == "row" and all(a ^ b == 3 for a, b in pairs):
        odd = lax.ppermute(even, axis, [(n, n ^ 2) for n in range(size)])
    else:
        odd = lax.ppermute(block, axis, route)
    return [even, odd]


def after(block, others):
    return call(
        pass_kernel,
        jax.ShapeDtypeStruct(block.shape, block.dtype),
        [VMEM] + [ANY] * len(others),
        VMEM,
        [],
        "after_others",
        0,
        0,
    )(block, *others)


def gather_metrics(packed, cores, units, first, second):
    order = ring_order(units)
    forward = [
        (order[n] * cores + k, order[(n + 1) % units] * cores + k)
        for n in range(units)
        for k in range(cores)
    ]
    backward = [(b, a) for a, b in forward]
    turns = [packed] + [None] * (units - 1)
    up = down = packed
    for step in range(1, units // 2 + 1):
        if step == 2 and first:
            up = after(up, first)
        up = lax.ppermute(up, "col", forward)
        if step == 2 and second:
            up = after(up, second)
        turns[step] = up
        if units - step > units // 2:
            down = lax.ppermute(down, "col", backward)
            turns[units - step] = down
    buffers = []
    for turn in turns:
        buffers.append(turn)
        for side in range(1, cores):
            swap = [
                (u * cores + k, u * cores + (k + side) % cores)
                for u in range(units)
                for k in range(cores)
            ]
            buffers.append(lax.ppermute(turn, "col", swap))
    return buffers


def spread(piece, sources, column_count, row_count, first):
    rows, columns = lax.axis_size("row"), len(sources)
    bits = rows.bit_length() - 1
    assert rows == 1 << bits
    reached = [[0] for _ in range(bits)]
    for step in range(bits):
        pairs, takers = [], []
        for turn in range(bits):
            bit = 1 << ((turn + step) % bits)
            pairs += [
                (row * columns + c, (row ^ bit) * columns + c)
                for c in range(turn, columns, bits)
                for row in range(rows)
            ]
            takers.append([away ^ bit for away in reached[turn]])
            reached[turn] = reached[turn] + takers[turn]
        got = lax.ppermute(piece, ("row", "col"), pairs)
        if step < bits - 1:
            piece = call(
                functools.partial(merge_kernel, takers, column_count, row_count),
                jax.ShapeDtypeStruct(piece.shape, piece.dtype),
                [VMEM, VMEM] + [ANY] * len(first),
                VMEM,
                [],
                "merge",
                0,
                0,
            )(piece, got, *first)
    return piece, got, takers


def on_device(
    fitting,
    coefficients,
    amplitudes,
    intersections,
    virtual_energy,
    occupied_energy,
    kept_count,
    orbital_atoms,
    fock_partner,
    fock_value,
):
    row_count, column_count = amplitudes.shape[:2]
    held, aux, pao = fitting.shape
    domain = orbital_atoms.shape[1]
    npno = virtual_energy.shape[2]
    terms = intersections.shape[2]
    columns = lax.axis_size("col")
    cores = row_count // column_count
    units = columns // cores
    scale = (2 * domain * aux) ** (-0.5)
    depth = pao + EXTRA
    half = pao // 2

    chunks = npno // 2
    lanes = 2 * npno
    atoms_table, fit, own_block, partner, value, occupied, virtual, coefs, inter, kept = [
        pltpu.with_memory_space_constraint(array, pltpu.HBM)
        for array in (
            orbital_atoms.T,
            fitting,
            amplitudes,
            fock_partner.T,
            fock_value.T,
            occupied_energy,
            virtual_energy,
            coefficients,
            intersections,
            kept_count.T,
        )
    ]
    packed, table, lines = call(
        pack_kernel,
        (
            jax.ShapeDtypeStruct((held, depth, half), BF16),
            jax.ShapeDtypeStruct(atoms_table.shape, jnp.int32),
            jax.ShapeDtypeStruct((row_count, column_count, chunks, lanes), BF16),
        ),
        [HBM] * 3,
        (VMEM,) * 3,
        [
            pltpu.VMEM(fitting.shape, BF16),
            pltpu.VMEM(amplitudes.shape, BF16),
            pltpu.VMEM((row_count, chunks, column_count, lanes), F32),
            pltpu.SemaphoreType.DMA((held,)),
            pltpu.SemaphoreType.DMA(()),
            pltpu.SemaphoreType.DMA(()),
        ],
        "pack_metric",
        2 * held * aux * pao * pao,
        fitting.size * 2,
    )(atoms_table, own_block, fit)
    row_halos = neighbours(lines, "row")
    col_halos = neighbours(lines, "col")
    shape = (row_count, column_count, domain, pao, lanes)
    own_coefficients, column_coefficients, own_turned, turned = call(
        prepare_kernel,
        (
            jax.ShapeDtypeStruct(shape, BF16),
            jax.ShapeDtypeStruct(shape, BF16),
            jax.ShapeDtypeStruct((row_count, domain, column_count * npno, pao), BF16),
            jax.ShapeDtypeStruct((column_count, domain, row_count * npno, pao), BF16),
        ),
        [HBM],
        (VMEM,) * 4,
        [pltpu.SemaphoreType.DMA((row_count,)), pltpu.SemaphoreType.DMA((row_count,))],
        "prepare",
        0,
        coefficients.size * 4,
    )(coefs)
    buffers = gather_metrics(packed, cores, units, row_halos[:1], [own_turned] + row_halos[1:])
    blocks = [lines] + row_halos + col_halos
    wanted = column_count * domain
    atoms = len(buffers) * held
    piece, metrics = call(
        functools.partial(select_kernel, cores, units),
        tuple(jax.ShapeDtypeStruct((n, depth, half), BF16) for n in (wanted, atoms)),
        [SMEM] + [VMEM] * len(buffers),
        (VMEM,) * 2,
        [],
        "select_column_atoms",
        0,
        (wanted + 2 * atoms) * depth * half * 4,
    )(table, *buffers)
    exchange = call(
        functools.partial(row_kernel, cores, units, held, scale),
        jax.ShapeDtypeStruct((row_count, column_count, npno, npno), F32),
        [SMEM] + [VMEM] * 3,
        VMEM,
        [pltpu.VMEM((domain, pao, pao), BF16)],
        "row_exchange",
        2 * row_count * column_count * domain * pao * npno * (pao + npno),
        coefficients.size,
    )(table, own_coefficients, own_turned, metrics)

    sources = [c * column_count // row_count for c in range(columns)]
    piece, got, takers = spread(piece, sources, column_count, row_count, [exchange] + col_halos)

    base = call(
        couple_kernel,
        jax.ShapeDtypeStruct((row_count, column_count, npno, npno), F32),
        [HBM] * 5 + [VMEM] * (1 + len(blocks)),
        VMEM,
        [
            pltpu.VMEM((chunks, terms, lanes), F32),
            pltpu.VMEM((npno, lanes), F32),
            pltpu.VMEM((len(blocks) * row_count, column_count, npno, npno), BF16),
            pltpu.VMEM((terms, npno, npno), BF16),
            pltpu.VMEM(intersections.shape, BF16),
            pltpu.SMEM(fock_partner.shape[::-1], jnp.int32),
            pltpu.SMEM(fock_value.shape[::-1], F32),
            pltpu.SMEM(occupied_energy.shape, F32),
            pltpu.VMEM(virtual_energy.shape, F32),
            pltpu.SemaphoreType.DMA((4,)),
            pltpu.SemaphoreType.DMA((row_count,)),
        ],
        "couple",
        4 * row_count * column_count * terms * npno**3,
        intersections.size * 4,
    )(partner, value, occupied, virtual, inter, exchange, *blocks)

    return call(
        functools.partial(column_kernel, takers, scale),
        jax.ShapeDtypeStruct(amplitudes.shape, F32),
        [HBM] + [VMEM] * 5,
        VMEM,
        [
            pltpu.VMEM((wanted, depth, half), BF16),
            pltpu.VMEM((wanted, pao, pao), BF16),
            pltpu.VMEM((row_count, column_count, npno, lanes), F32),
            pltpu.VMEM((row_count, column_count, chunks, lanes), F32),
            pltpu.SMEM(kept_count.shape[::-1], jnp.int32),
            pltpu.SemaphoreType.DMA(()),
        ],
        "column_exchange",
        2 * row_count * column_count * domain * pao * npno * (pao + npno),
        coefficients.size,
    )(kept, column_coefficients, turned, base, piece, got)


def solution(mesh):
    placed = (
        P(("row", "col"), None, None),
        P("row", "col", None, None, None),
        P("row", "col", None),
        P("row", "col", None, None),
        P("row", "col", None),
        P(),
        P("row", "col"),
        P(),
        P(),
        P(),
    )
    return jax.shard_map(
        on_device, mesh=mesh, in_specs=placed, out_specs=P("row", "col", None), check_vma=False
    )
```

```python
import functools

import jax
import jax.numpy as jnp
from jax import lax
from jax.experimental import pallas as pl
from jax.experimental.pallas import tpu as pltpu
from jax.sharding import PartitionSpec as P

F32 = jnp.float32
BF16 = jnp.bfloat16
EXTRA = 16
VMEM = pl.BlockSpec(memory_space=pltpu.VMEM)
SMEM = pl.BlockSpec(memory_space=pltpu.SMEM)
HBM = pl.BlockSpec(memory_space=pltpu.HBM)
ANY = pl.BlockSpec(memory_space=pl.ANY)


def dot(a, b):
    return jnp.dot(a, b, preferred_element_type=F32)


def dot_nt(a, b):
    return lax.dot_general(a, b, (((1,), (1,)), ((), ())), preferred_element_type=F32)


def square_iota(n):
    return (
        lax.broadcasted_iota(jnp.int32, (n, n), 0),
        lax.broadcasted_iota(jnp.int32, (n, n), 1),
    )


def pack_kernel(
    atoms_ref, block_hbm, fit_ref, out_ref, table_ref, lines_ref,
    fits_ref, block_ref, flat_ref, sems, table_sem, block_sem,
):
    held = fit_ref.shape[0]
    half = fit_ref.shape[2] // 2
    row, col = square_iota(half)
    place = lax.broadcasted_iota(jnp.int32, (EXTRA, half), 0)
    fetches = [
        pltpu.make_async_copy(fit_ref.at[atom], fits_ref.at[atom], sems.at[atom])
        for atom in range(held)
    ]
    block = pltpu.make_async_copy(block_hbm, block_ref, block_sem)
    block.start()
    for fetch in fetches:
        fetch.start()
    table = pltpu.make_async_copy(atoms_ref, table_ref, table_sem)
    table.start()
    block.wait()
    row_count, column_count, chunks, lanes = lines_ref.shape
    for i in range(row_count):
        for q in range(chunks):
            flat_ref[i, q] = block_ref[i, :, q * lanes : (q + 1) * lanes].astype(F32)
    for i in range(row_count):
        for j in range(column_count):
            lines_ref[i, j] = flat_ref[i, :, j, :].astype(BF16)
    for fetch in fetches:
        fetch.wait()
    for atom in range(held):
        fit = fits_ref[atom]
        metric = lax.dot_general(fit, fit, (((0,), (0,)), ((), ())), preferred_element_type=F32)
        first, second = metric[:half, :half], metric[half:, half:]
        out_ref[atom, :half] = metric[:half, half:].astype(BF16)
        out_ref[atom, half : 2 * half] = jnp.where(row <= col, first, second).astype(BF16)
        lines = [jnp.sum(jnp.where(row == col, m, 0.0), axis=0, keepdims=True) for m in (first, second)]
        high = [line.astype(BF16).astype(F32) for line in lines]
        extra = jnp.where(
            place == 0,
            high[1],
            jnp.where(
                place == 1,
                lines[0] - high[0],
                jnp.where(place == 2, lines[1] - high[1], 0.0),
            ),
        )
        out_ref[atom, 2 * half :] = extra.astype(BF16)
    table.wait()


def unpack(packed, metric_ref):
    half = packed.shape[1]
    row, col = square_iota(half)
    corner = packed[:half]
    both = packed[half : 2 * half].astype(F32)
    extra = packed[2 * half :].astype(F32)
    turned = both.T
    metric_ref[:half, :half] = jnp.where(row <= col, both, turned).astype(BF16)
    metric_ref[:half, half:] = corner
    metric_ref[half:, :half] = corner.astype(F32).T.astype(BF16)
    metric_ref[half:, half:] = jnp.where(
        row > col, both, jnp.where(row == col, extra[0:1], turned)
    ).astype(BF16)
    return jnp.concatenate([extra[1:2], extra[2:3]], axis=1)


def ring_order(units):
    return [0] + list(range(1, units, 2)) + list(range(units - units % 2 - (0 if units % 2 else 2), 0, -2))


def ring_place(unit, units):
    return jnp.where(unit % 2 == 1, (unit + 1) // 2, (units - unit // 2) % units)


def pick_place(atom, row_place, col_place, cores, units, held):
    label = jnp.clip(atom - row_place * (units * cores * held), 0, units * cores * held - 1)
    owner, slot = label // held, label % held
    turn = (ring_place(col_place // cores, units) - ring_place(owner // cores, units) + units) % units
    side = (col_place % cores - owner % cores + cores) % cores
    return (turn * cores + side) * held + slot


def select_kernel(cores, units, atoms_ref, *refs):
    count = units * cores
    buffers, (piece_ref, all_ref) = refs[:count], refs[-2:]
    held = buffers[0].shape[0]
    row_place, col_place = lax.axis_index("row"), lax.axis_index("col")
    domain = atoms_ref.shape[0]
    wanted = piece_ref.shape[0]
    for index, buffer in enumerate(buffers):
        all_ref[index * held : (index + 1) * held] = buffer[...]
    for index in range(wanted):
        atom = atoms_ref[index % domain, col_place * (wanted // domain) + index // domain]
        place = pick_place(atom, row_place, col_place, cores, units, held)
        piece_ref[index] = all_ref[place]


def pass_kernel(block_ref, *refs):
    refs[-1][...] = block_ref[...]


def neighbour_place(place, turn):
    return jnp.where(turn == 0, 0, jnp.where((place + turn) == jnp.bitwise_xor(place, 1), 1, 2))


def couple_kernel(scale, partner_hbm, value_hbm, occupied_hbm, virtual_hbm, kept_hbm, inter_hbm, *refs):
    exchange_ref, blocks = refs[0], refs[1:6]
    base_ref, factor_ref, flat_ref, wide_ref, mats_ref, inters_ref, inter_ref = refs[6:13]
    partner_ref, value_ref, occupied_ref, virtual_ref, kept_ref, sems, inter_sems = refs[13:]
    row_count, column_count, terms, size = inter_ref.shape
    chunks, lanes = base_ref.shape[2:]
    npno = lanes // 2
    partners = terms // 2
    row_place, col_place = lax.axis_index("row"), lax.axis_index("col")
    first_row = row_place * row_count
    first_col = col_place * column_count
    fetches = [
        pltpu.make_async_copy(source, target, sems.at[n])
        for n, (source, target) in enumerate(
            [
                (partner_hbm, partner_ref),
                (value_hbm, value_ref),
                (occupied_hbm, occupied_ref),
                (virtual_hbm, virtual_ref),
                (kept_hbm, kept_ref),
            ]
        )
    ]

    def fetch_inter(i):
        return pltpu.make_async_copy(inter_hbm.at[i], inter_ref.at[i], inter_sems.at[i])

    for fetch in fetches:
        fetch.start()
    for i in range(row_count):
        fetch_inter(i).start()
    def square(lines):
        wide_ref[pl.ds(0, chunks, 2), :] = lines
        wide_ref[pl.ds(1, chunks, 2), :] = pltpu.roll(lines, npno, 1)
        return wide_ref[:, :npno]

    for index, block in enumerate(blocks):

        def one_block(i, carry, index=index, block=block):
            for j in range(column_count):
                mats_ref[index * row_count + i, j] = square(block[i, j].astype(F32)).astype(BF16)
            return carry

        lax.fori_loop(0, row_count, one_block, 0)
    for fetch in fetches:
        fetch.wait()

    place = lax.broadcasted_iota(jnp.int32, (chunks, lanes), 0)
    lane = lax.broadcasted_iota(jnp.int32, (chunks, lanes), 1)
    first = 2 * place + jnp.where(lane < npno, 0, 1)
    second = jnp.where(lane < npno, lane, lane - npno)

    def one_row(i, carry):
        fetch_inter(i).wait()
        for j in range(column_count):
            for q in range(chunks):
                flat_ref[q] = inter_ref[i, j, :, q * lanes : (q + 1) * lanes].astype(F32)
            turned = []
            for n in range(terms):
                inter = square(flat_ref[:, n, :])
                inters_ref[n] = inter.astype(BF16)
                turned.append(inter.T.astype(BF16))
            total = jnp.zeros((npno, npno), F32)
            for n in range(terms):
                if n < partners:
                    away = partner_ref[n, first_row + i] - first_row + row_count
                    turn = away // row_count - 1
                    index = neighbour_place(row_place, turn) * row_count + away % row_count
                    weight = value_ref[n, first_row + i]
                    partner = mats_ref[index, j]
                else:
                    away = partner_ref[n - partners, first_col + j] - first_col + column_count
                    turn = away // column_count - 1
                    index = neighbour_place(col_place, turn)
                    index = jnp.where(index == 0, 0, index + 2) * row_count + i
                    weight = value_ref[n - partners, first_col + j]
                    partner = mats_ref[index, away % column_count]
                half = dot(inters_ref[n], partner).astype(BF16)
                total = total + weight * dot(half, turned[n])
            levels = jnp.broadcast_to(virtual_ref[i, pl.ds(j, 1)], (npno, npno))
            shift = levels + levels.T - occupied_ref[first_row + i] - occupied_ref[first_col + j]
            result = exchange_ref[i, j] + shift * mats_ref[i, j].astype(F32) - total
            wide_ref[:, :npno] = result
            even = wide_ref[pl.ds(0, chunks, 2), :]
            odd = pltpu.roll(wide_ref[pl.ds(1, chunks, 2), :], npno, 1)
            keep = (first < kept_ref[j, i]) & (second < kept_ref[j, i])
            base_ref[i, j] = jnp.where(keep, jnp.where(lane < npno, even, odd), 0.0)
            factor_ref[i, j] = jnp.where(keep, scale, 0.0)
        return carry

    lax.fori_loop(0, row_count, one_row, 0)


def prepare_kernel(coef_hbm, own_ref, coef_ref, own_turned_ref, turned_ref, own_sems, coef_sems):
    row_count, column_count, domain, _, lanes = own_ref.shape
    npno = lanes // 2

    def fetch(i, first, target_ref, sems):
        return pltpu.make_async_copy(
            coef_hbm.at[i, :, pl.ds(first, domain)], target_ref.at[i], sems.at[i]
        )

    for i in range(row_count):
        fetch(i, 0, own_ref, own_sems).start()
        fetch(i, domain, coef_ref, coef_sems).start()
    for i in range(row_count):
        fetch(i, 0, own_ref, own_sems).wait()
        for j in range(column_count):
            for s in range(domain):
                own_turned_ref[i, s, j * npno : (j + 1) * npno] = own_ref[i, j, s].T[:npno]
        fetch(i, domain, coef_ref, coef_sems).wait()
        for j in range(column_count):
            for s in range(domain):
                turned_ref[j, s, i * npno : (i + 1) * npno] = coef_ref[i, j, s].T[:npno]


def row_kernel(cores, units, held, scale, atoms_ref, coef_ref, turned_ref, all_ref, out_ref, metric_ref):
    row_count, column_count, domain = coef_ref.shape[:3]
    npno = out_ref.shape[2]
    row_place, col_place = lax.axis_index("row"), lax.axis_index("col")

    def one_row(i, carry):
        lows = []
        for s in range(domain):
            atom = atoms_ref[s, row_place * row_count + i]
            place = pick_place(atom, row_place, col_place, cores, units, held)
            lows.append(unpack(all_ref[place], metric_ref.at[s]))
        products = []
        for s in range(domain):
            left = turned_ref[i, s]
            product = dot(left, metric_ref[s]) + left.astype(F32) * lows[s]
            products.append(product.astype(BF16))
        for j in range(column_count):
            total = dot(products[0][j * npno : (j + 1) * npno], coef_ref[i, j, 0])
            for s in range(1, domain):
                total = total + dot(products[s][j * npno : (j + 1) * npno], coef_ref[i, j, s])
            out_ref[i, j] = total[:, npno:] * scale
        return carry

    lax.fori_loop(0, row_count, one_row, 0)


def merge_into(takers, column_count, row_count, kept, got, target):
    col_place = lax.axis_index("col")
    away = jnp.bitwise_xor(lax.axis_index("row"), col_place * column_count // row_count)
    turn = col_place % len(takers)
    taken = functools.reduce(
        jnp.logical_or,
        [(turn == n) & (away == taker) for n, these in enumerate(takers) for taker in these],
    )

    @pl.when(taken)
    def _():
        target[...] = got[...]

    @pl.when(jnp.logical_not(taken))
    def _():
        target[...] = kept[...]


def merge_kernel(takers, column_count, row_count, kept_ref, got_ref, *refs):
    merge_into(takers, column_count, row_count, kept_ref, got_ref, refs[-1])


def column_kernel(
    takers, coef_ref, turned_ref, base_ref, factor_ref, held_ref, got_ref,
    out_hbm, packed_ref, metric_ref, wide_ref, flat_ref, out_ref, sems,
):
    row_count, column_count, domain, pao, lanes = coef_ref.shape
    npno = lanes // 2
    chunks = npno // 2
    merge_into(takers, column_count, row_count, held_ref, got_ref, packed_ref)
    slots = column_count * domain
    lows = [unpack(packed_ref[index], metric_ref.at[index]) for index in range(slots)]
    products = []
    for j in range(column_count):
        parts = []
        for s in range(domain):
            left = turned_ref[j, s]
            part = dot(left, metric_ref[j * domain + s]) + left.astype(F32) * lows[j * domain + s]
            parts.append(part.astype(BF16))
        products.append(jnp.concatenate(parts, axis=1))
    lane = lax.broadcasted_iota(jnp.int32, (chunks, lanes), 1)
    for i in range(row_count):
        for j in range(column_count):
            wide_ref[i, j] = dot(
                products[j][i * npno : (i + 1) * npno], coef_ref[i, j].reshape(domain * pao, lanes)
            )
            even = wide_ref[i, j, pl.ds(0, chunks, 2), :]
            odd = wide_ref[i, j, pl.ds(1, chunks, 2), :]
            total = jnp.where(lane < npno, pltpu.roll(even, npno, 1), odd)
            flat_ref[i, j] = base_ref[i, j] + factor_ref[i, j] * total
        for q in range(chunks):
            out_ref[i, :, q * lanes : (q + 1) * lanes] = flat_ref[i, :, q, :]
        pltpu.make_async_copy(out_ref.at[i], out_hbm.at[i], sems.at[i]).start()
    for i in range(row_count):
        pltpu.make_async_copy(out_ref.at[i], out_hbm.at[i], sems.at[i]).wait()


def call(kernel, out_shape, in_specs, out_specs, scratch, name, flops, moved):
    return pl.pallas_call(
        kernel,
        out_shape=out_shape,
        in_specs=in_specs,
        out_specs=out_specs,
        scratch_shapes=scratch,
        compiler_params=pltpu.CompilerParams(vmem_limit_bytes=48 * 2**20),
        cost_estimate=pl.CostEstimate(flops=flops, bytes_accessed=moved, transcendentals=0),
        name=name,
    )


def partners_of(size, first):
    pairs = [(n, n + 1) for n in range(first, size - 1, 2)]
    alone = [(n, n) for n in range(size) if n < first or n >= first + 2 * len(pairs)]
    return pairs, pairs + [(b, a) for a, b in pairs] + alone


def neighbours(block, axis):
    size = lax.axis_size(axis)
    even = lax.ppermute(block, axis, partners_of(size, 0)[1])
    pairs, route = partners_of(size, 1)
    if size % 4 == 0 and axis == "row" and all(a ^ b == 3 for a, b in pairs):
        odd = lax.ppermute(block, axis, [(n, n ^ 3) for n in range(size)])
    else:
        odd = lax.ppermute(block, axis, route)
    return [even, odd]


def after(block, others):
    return call(
        pass_kernel,
        jax.ShapeDtypeStruct(block.shape, block.dtype),
        [VMEM] + [ANY] * len(others),
        VMEM,
        [],
        "after_others",
        0,
        0,
    )(block, *others)


def gather_metrics(packed, cores, units, first, second):
    order = ring_order(units)
    forward = [
        (order[n] * cores + k, order[(n + 1) % units] * cores + k)
        for n in range(units)
        for k in range(cores)
    ]
    backward = [(b, a) for a, b in forward]
    turns = [packed] + [None] * (units - 1)
    up = down = packed
    for step in range(1, units // 2 + 1):
        if step == 2 and first:
            up = after(up, first)
        up = lax.ppermute(up, "col", forward)
        if step == 2 and second:
            up = after(up, second)
        turns[step] = up
        if units - step > units // 2:
            down = lax.ppermute(down, "col", backward)
            turns[units - step] = down
    buffers = []
    for turn in turns:
        buffers.append(turn)
        for side in range(1, cores):
            swap = [
                (u * cores + k, u * cores + (k + side) % cores)
                for u in range(units)
                for k in range(cores)
            ]
            buffers.append(lax.ppermute(turn, "col", swap))
    return buffers


def spread(piece, sources, column_count, row_count, first):
    rows, columns = lax.axis_size("row"), len(sources)
    bits = rows.bit_length() - 1
    assert rows == 1 << bits
    reached = [[0] for _ in range(bits)]
    for step in range(bits):
        pairs, takers = [], []
        for turn in range(bits):
            bit = 1 << ((turn + step) % bits)
            pairs += [
                (row * columns + c, (row ^ bit) * columns + c)
                for c in range(turn, columns, bits)
                for row in range(rows)
            ]
            takers.append([away ^ bit for away in reached[turn]])
            reached[turn] = reached[turn] + takers[turn]
        got = lax.ppermute(piece, ("row", "col"), pairs)
        if step < bits - 1:
            piece = call(
                functools.partial(merge_kernel, takers, column_count, row_count),
                jax.ShapeDtypeStruct(piece.shape, piece.dtype),
                [VMEM, VMEM] + [ANY] * len(first),
                VMEM,
                [],
                "merge",
                0,
                0,
            )(piece, got, *first)
    return piece, got, takers


def on_device(
    fitting,
    coefficients,
    amplitudes,
    intersections,
    virtual_energy,
    occupied_energy,
    kept_count,
    orbital_atoms,
    fock_partner,
    fock_value,
):
    row_count, column_count = amplitudes.shape[:2]
    held, aux, pao = fitting.shape
    domain = orbital_atoms.shape[1]
    npno = virtual_energy.shape[2]
    terms = intersections.shape[2]
    columns = lax.axis_size("col")
    cores = row_count // column_count
    units = columns // cores
    scale = (2 * domain * aux) ** (-0.5)
    depth = pao + EXTRA
    half = pao // 2

    chunks = npno // 2
    lanes = 2 * npno
    atoms_table, fit, own_block, partner, value, occupied, virtual, coefs, inter, kept = [
        pltpu.with_memory_space_constraint(array, pltpu.HBM)
        for array in (
            orbital_atoms.T,
            fitting,
            amplitudes,
            fock_partner.T,
            fock_value.T,
            occupied_energy,
            virtual_energy,
            coefficients,
            intersections,
            kept_count.T,
        )
    ]
    packed, table, lines = call(
        pack_kernel,
        (
            jax.ShapeDtypeStruct((held, depth, half), BF16),
            jax.ShapeDtypeStruct(atoms_table.shape, jnp.int32),
            jax.ShapeDtypeStruct((row_count, column_count, chunks, lanes), BF16),
        ),
        [HBM] * 3,
        (VMEM,) * 3,
        [
            pltpu.VMEM(fitting.shape, BF16),
            pltpu.VMEM(amplitudes.shape, BF16),
            pltpu.VMEM((row_count, chunks, column_count, lanes), F32),
            pltpu.SemaphoreType.DMA((held,)),
            pltpu.SemaphoreType.DMA(()),
            pltpu.SemaphoreType.DMA(()),
        ],
        "pack_metric",
        2 * held * aux * pao * pao,
        fitting.size * 2,
    )(atoms_table, own_block, fit)
    row_halos = neighbours(lines, "row")
    col_halos = neighbours(lines, "col")
    shape = (row_count, column_count, domain, pao, lanes)
    own_coefficients, column_coefficients, own_turned, turned = call(
        prepare_kernel,
        (
            jax.ShapeDtypeStruct(shape, BF16),
            jax.ShapeDtypeStruct(shape, BF16),
            jax.ShapeDtypeStruct((row_count, domain, column_count * npno, pao), BF16),
            jax.ShapeDtypeStruct((column_count, domain, row_count * npno, pao), BF16),
        ),
        [HBM],
        (VMEM,) * 4,
        [pltpu.SemaphoreType.DMA((row_count,)), pltpu.SemaphoreType.DMA((row_count,))],
        "prepare",
        0,
        coefficients.size * 4,
    )(coefs)
    buffers = gather_metrics(packed, cores, units, row_halos, [own_turned])
    blocks = [lines] + row_halos + col_halos
    wanted = column_count * domain
    atoms = len(buffers) * held
    piece, metrics = call(
        functools.partial(select_kernel, cores, units),
        tuple(jax.ShapeDtypeStruct((n, depth, half), BF16) for n in (wanted, atoms)),
        [SMEM] + [VMEM] * len(buffers),
        (VMEM,) * 2,
        [],
        "select_column_atoms",
        0,
        (wanted + 2 * atoms) * depth * half * 4,
    )(table, *buffers)
    exchange = call(
        functools.partial(row_kernel, cores, units, held, scale),
        jax.ShapeDtypeStruct((row_count, column_count, npno, npno), F32),
        [SMEM] + [VMEM] * 3,
        VMEM,
        [pltpu.VMEM((domain, pao, pao), BF16)],
        "row_exchange",
        2 * row_count * column_count * domain * pao * npno * (pao + npno),
        coefficients.size,
    )(table, own_coefficients, own_turned, metrics)

    sources = [c * column_count // row_count for c in range(columns)]
    piece, got, takers = spread(piece, sources, column_count, row_count, [exchange] + col_halos)

    base, factor = call(
        functools.partial(couple_kernel, scale),
        (jax.ShapeDtypeStruct((row_count, column_count, chunks, lanes), F32),) * 2,
        [HBM] * 6 + [VMEM] * (1 + len(blocks)),
        (VMEM,) * 2,
        [
            pltpu.VMEM((chunks, terms, lanes), F32),
            pltpu.VMEM((npno, lanes), F32),
            pltpu.VMEM((len(blocks) * row_count, column_count, npno, npno), BF16),
            pltpu.VMEM((terms, npno, npno), BF16),
            pltpu.VMEM(intersections.shape, BF16),
            pltpu.SMEM(fock_partner.shape[::-1], jnp.int32),
            pltpu.SMEM(fock_value.shape[::-1], F32),
            pltpu.SMEM(occupied_energy.shape, F32),
            pltpu.VMEM(virtual_energy.shape, F32),
            pltpu.SMEM(kept_count.shape[::-1], jnp.int32),
            pltpu.SemaphoreType.DMA((5,)),
            pltpu.SemaphoreType.DMA((row_count,)),
        ],
        "couple",
        4 * row_count * column_count * terms * npno**3,
        intersections.size * 4,
    )(partner, value, occupied, virtual, kept, inter, exchange, *blocks)

    return call(
        functools.partial(column_kernel, takers),
        jax.ShapeDtypeStruct(amplitudes.shape, F32),
        [VMEM] * 6,
        HBM,
        [
            pltpu.VMEM((wanted, depth, half), BF16),
            pltpu.VMEM((wanted, pao, pao), BF16),
            pltpu.VMEM((row_count, column_count, npno, lanes), F32),
            pltpu.VMEM((row_count, column_count, chunks, lanes), F32),
            pltpu.VMEM(amplitudes.shape, F32),
            pltpu.SemaphoreType.DMA((row_count,)),
        ],
        "column_exchange",
        2 * row_count * column_count * domain * pao * npno * (pao + npno),
        coefficients.size,
    )(column_coefficients, turned, base, factor, piece, got)


def solution(mesh):
    placed = (
        P(("row", "col"), None, None),
        P("row", "col", None, None, None),
        P("row", "col", None),
        P("row", "col", None, None),
        P("row", "col", None),
        P(),
        P("row", "col"),
        P(),
        P(),
        P(),
    )
    return jax.shard_map(
        on_device, mesh=mesh, in_specs=placed, out_specs=P("row", "col", None), check_vma=False
    )
```

```python
import functools

import jax
import jax.numpy as jnp
from jax import lax
from jax.experimental import pallas as pl
from jax.experimental.pallas import tpu as pltpu
from jax.sharding import PartitionSpec as P

F32 = jnp.float32
BF16 = jnp.bfloat16
EXTRA = 16
VMEM = pl.BlockSpec(memory_space=pltpu.VMEM)
SMEM = pl.BlockSpec(memory_space=pltpu.SMEM)
HBM = pl.BlockSpec(memory_space=pltpu.HBM)
ANY = pl.BlockSpec(memory_space=pl.ANY)


def dot(a, b):
    return jnp.dot(a, b, preferred_element_type=F32)


def dot_nt(a, b):
    return lax.dot_general(a, b, (((1,), (1,)), ((), ())), preferred_element_type=F32)


def square_iota(n):
    return (
        lax.broadcasted_iota(jnp.int32, (n, n), 0),
        lax.broadcasted_iota(jnp.int32, (n, n), 1),
    )


def pack_kernel(
    atoms_ref, block_hbm, fit_ref, out_ref, table_ref, lines_ref,
    fits_ref, block_ref, flat_ref, sems, table_sem, block_sem,
):
    held = fit_ref.shape[0]
    half = fit_ref.shape[2] // 2
    row, col = square_iota(half)
    place = lax.broadcasted_iota(jnp.int32, (EXTRA, half), 0)
    fetches = [
        pltpu.make_async_copy(fit_ref.at[atom], fits_ref.at[atom], sems.at[atom])
        for atom in range(held)
    ]
    block = pltpu.make_async_copy(block_hbm, block_ref, block_sem)
    block.start()
    for fetch in fetches:
        fetch.start()
    table = pltpu.make_async_copy(atoms_ref, table_ref, table_sem)
    table.start()
    block.wait()
    row_count, column_count, chunks, lanes = lines_ref.shape
    for i in range(row_count):
        for q in range(chunks):
            flat_ref[i, q] = block_ref[i, :, q * lanes : (q + 1) * lanes].astype(F32)
    for i in range(row_count):
        for j in range(column_count):
            lines_ref[i, j] = flat_ref[i, :, j, :].astype(BF16)
    for fetch in fetches:
        fetch.wait()
    for atom in range(held):
        fit = fits_ref[atom]
        metric = lax.dot_general(fit, fit, (((0,), (0,)), ((), ())), preferred_element_type=F32)
        first, second = metric[:half, :half], metric[half:, half:]
        out_ref[atom, :half] = metric[:half, half:].astype(BF16)
        out_ref[atom, half : 2 * half] = jnp.where(row <= col, first, second).astype(BF16)
        lines = [jnp.sum(jnp.where(row == col, m, 0.0), axis=0, keepdims=True) for m in (first, second)]
        high = [line.astype(BF16).astype(F32) for line in lines]
        extra = jnp.where(
            place == 0,
            high[1],
            jnp.where(
                place == 1,
                lines[0] - high[0],
                jnp.where(place == 2, lines[1] - high[1], 0.0),
            ),
        )
        out_ref[atom, 2 * half :] = extra.astype(BF16)
    table.wait()


def unpack(packed, metric_ref):
    half = packed.shape[1]
    row, col = square_iota(half)
    corner = packed[:half]
    both = packed[half : 2 * half].astype(F32)
    extra = packed[2 * half :].astype(F32)
    turned = both.T
    metric_ref[:half, :half] = jnp.where(row <= col, both, turned).astype(BF16)
    metric_ref[:half, half:] = corner
    metric_ref[half:, :half] = corner.astype(F32).T.astype(BF16)
    metric_ref[half:, half:] = jnp.where(
        row > col, both, jnp.where(row == col, extra[0:1], turned)
    ).astype(BF16)
    return jnp.concatenate([extra[1:2], extra[2:3]], axis=1)


def ring_order(units):
    return [0] + list(range(1, units, 2)) + list(range(units - units % 2 - (0 if units % 2 else 2), 0, -2))


def ring_place(unit, units):
    return jnp.where(unit % 2 == 1, (unit + 1) // 2, (units - unit // 2) % units)


def pick_place(atom, row_place, col_place, cores, units, held):
    label = jnp.clip(atom - row_place * (units * cores * held), 0, units * cores * held - 1)
    owner, slot = label // held, label % held
    turn = (ring_place(col_place // cores, units) - ring_place(owner // cores, units) + units) % units
    side = (col_place % cores - owner % cores + cores) % cores
    return (turn * cores + side) * held + slot


def select_kernel(cores, units, atoms_ref, *refs):
    count = units * cores
    buffers, pieces, all_ref = refs[:count], refs[count:-1], refs[-1]
    held = buffers[0].shape[0]
    row_place, col_place = lax.axis_index("row"), lax.axis_index("col")
    for index, buffer in enumerate(buffers):
        all_ref[index * held : (index + 1) * held] = buffer[...]
    for j, piece_ref in enumerate(pieces):
        for s in range(piece_ref.shape[0]):
            atom = atoms_ref[s, col_place * len(pieces) + j]
            place = pick_place(atom, row_place, col_place, cores, units, held)
            piece_ref[s] = all_ref[place]


def pass_kernel(block_ref, *refs):
    refs[-1][...] = block_ref[...]


def neighbour_place(place, turn):
    return jnp.where(turn == 0, 0, jnp.where((place + turn) == jnp.bitwise_xor(place, 1), 1, 2))


def couple_kernel(
    partner_hbm, value_hbm, occupied_hbm, virtual_hbm, inter_ref, turned_ref, factor_ref, *refs,
):
    exchange_ref, blocks = refs[0], refs[1:6]
    base_ref, wide_ref, mats_ref = refs[6:9]
    partner_ref, value_ref, occupied_ref, virtual_ref, sems = refs[9:]
    row_count, column_count, terms, npno, _ = inter_ref.shape
    chunks, lanes = base_ref.shape[2:]
    partners = terms // 2
    row_place, col_place = lax.axis_index("row"), lax.axis_index("col")
    first_row = row_place * row_count
    first_col = col_place * column_count
    fetches = [
        pltpu.make_async_copy(source, target, sems.at[n])
        for n, (source, target) in enumerate(
            [
                (partner_hbm, partner_ref),
                (value_hbm, value_ref),
                (occupied_hbm, occupied_ref),
                (virtual_hbm, virtual_ref),
            ]
        )
    ]
    for fetch in fetches:
        fetch.start()

    for index, block in enumerate(blocks):
        for i in range(row_count):
            for j in range(column_count):
                lines = block[i, j].astype(F32)
                wide = wide_ref.at[(i * column_count + j) % wide_ref.shape[0]]
                wide[pl.ds(0, chunks, 2), :] = lines
                wide[pl.ds(1, chunks, 2), :] = pltpu.roll(lines, npno, 1)
                mats_ref[index * row_count + i, j] = wide[:, :npno].astype(BF16)
    for fetch in fetches:
        fetch.wait()
    lane = lax.broadcasted_iota(jnp.int32, (chunks, lanes), 1)

    def one_row(i, carry):
        for j in range(column_count):
            total = jnp.zeros((npno, npno), F32)
            for n in range(terms):
                if n < partners:
                    away = partner_ref[n, first_row + i] - first_row + row_count
                    turn = away // row_count - 1
                    index = neighbour_place(row_place, turn) * row_count + away % row_count
                    weight = value_ref[n, first_row + i]
                    partner = mats_ref[index, j]
                else:
                    away = partner_ref[n - partners, first_col + j] - first_col + column_count
                    turn = away // column_count - 1
                    index = neighbour_place(col_place, turn)
                    index = jnp.where(index == 0, 0, index + 2) * row_count + i
                    weight = value_ref[n - partners, first_col + j]
                    partner = mats_ref[index, away % column_count]
                half = dot(inter_ref[i, j, n], partner).astype(BF16)
                total = total + weight * dot(half, turned_ref[i, j, n])
            levels = jnp.broadcast_to(virtual_ref[i, pl.ds(j, 1)], (npno, npno))
            shift = levels + levels.T - occupied_ref[first_row + i] - occupied_ref[first_col + j]
            wide = wide_ref.at[j]
            wide[:, :npno] = exchange_ref[i, j] + shift * mats_ref[i, j].astype(F32) - total
            even = wide[pl.ds(0, chunks, 2), :]
            odd = pltpu.roll(wide[pl.ds(1, chunks, 2), :], npno, 1)
            result = jnp.where(lane < npno, even, odd)
            base_ref[i, j] = jnp.where(factor_ref[i, j] == 0.0, 0.0, result)
        return carry

    lax.fori_loop(0, row_count, one_row, 0)


def prepare_kernel(coef_hbm, own_ref, coef_ref, own_turned_ref, turned_ref, own_sems, coef_sems):
    row_count, column_count, domain, _, lanes = own_ref.shape
    npno = lanes // 2

    def fetch(i, first, target_ref, sems):
        return pltpu.make_async_copy(
            coef_hbm.at[i, :, pl.ds(first, domain)], target_ref.at[i], sems.at[i]
        )

    for i in range(row_count):
        fetch(i, 0, own_ref, own_sems).start()
        fetch(i, domain, coef_ref, coef_sems).start()
    for i in range(row_count):
        fetch(i, 0, own_ref, own_sems).wait()
        for j in range(column_count):
            for s in range(domain):
                own_turned_ref[i, s, j * npno : (j + 1) * npno] = own_ref[i, j, s].T[:npno]
        fetch(i, domain, coef_ref, coef_sems).wait()
        for j in range(column_count):
            for s in range(domain):
                turned_ref[j, s, i * npno : (i + 1) * npno] = coef_ref[i, j, s].T[:npno]


def square_kernel(
    scale, kept_hbm, inter_hbm, mats_ref, turned_mats_ref, factor_ref,
    inter_ref, flat_ref, wide_ref, kept_ref, inter_sems, kept_sem,
):
    row_count, column_count, terms, npno, _ = mats_ref.shape
    chunks, lanes = factor_ref.shape[2:]

    def fetch_inter(i):
        return pltpu.make_async_copy(inter_hbm.at[i], inter_ref.at[i], inter_sems.at[i])

    kept_copy = pltpu.make_async_copy(kept_hbm, kept_ref, kept_sem)
    kept_copy.start()
    for i in range(row_count):
        fetch_inter(i).start()

    def one_row(i, carry):
        fetch_inter(i).wait()
        for j in range(column_count):
            for q in range(chunks):
                flat_ref[j, q] = inter_ref[i, j, :, q * lanes : (q + 1) * lanes].astype(F32)
            for n in range(terms):
                lines = flat_ref[j, :, n, :]
                wide_ref[j, n, pl.ds(0, chunks, 2), :] = lines
                wide_ref[j, n, pl.ds(1, chunks, 2), :] = pltpu.roll(lines, npno, 1)
        for j in range(column_count):
            for n in range(terms):
                inter = wide_ref[j, n, :, :npno]
                mats_ref[i, j, n] = inter.astype(BF16)
                turned_mats_ref[i, j, n] = inter.T.astype(BF16)
        return carry

    lax.fori_loop(0, row_count, one_row, 0)
    kept_copy.wait()
    place = lax.broadcasted_iota(jnp.int32, (chunks, lanes), 0)
    lane = lax.broadcasted_iota(jnp.int32, (chunks, lanes), 1)
    first = 2 * place + jnp.where(lane < npno, 0, 1)
    second = jnp.where(lane < npno, lane, lane - npno)
    most = jnp.maximum(first, second)
    for i in range(row_count):
        for j in range(column_count):
            factor_ref[i, j] = jnp.where(most < kept_ref[j, i], scale, 0.0)


def row_kernel(cores, units, held, scale, atoms_ref, coef_ref, turned_ref, all_ref, out_ref, metric_ref):
    row_count, column_count, domain = coef_ref.shape[:3]
    npno = out_ref.shape[2]
    row_place, col_place = lax.axis_index("row"), lax.axis_index("col")

    def one_row(i, carry):
        lows = []
        for s in range(domain):
            atom = atoms_ref[s, row_place * row_count + i]
            place = pick_place(atom, row_place, col_place, cores, units, held)
            lows.append(unpack(all_ref[place], metric_ref.at[s]))
        products = []
        for s in range(domain):
            left = turned_ref[i, s]
            product = dot(left, metric_ref[s]) + left.astype(F32) * lows[s]
            products.append(product.astype(BF16))
        for j in range(column_count):
            total = dot(products[0][j * npno : (j + 1) * npno], coef_ref[i, j, 0])
            for s in range(1, domain):
                total = total + dot(products[s][j * npno : (j + 1) * npno], coef_ref[i, j, s])
            out_ref[i, j] = total[:, npno:] * scale
        return carry

    lax.fori_loop(0, row_count, one_row, 0)


def merge_into(takers, column_count, row_count, kept, got, target):
    col_place = lax.axis_index("col")
    away = jnp.bitwise_xor(lax.axis_index("row"), col_place * column_count // row_count)
    turn = col_place % len(takers)
    taken = functools.reduce(
        jnp.logical_or,
        [(turn == n) & (away == taker) for n, these in enumerate(takers) for taker in these],
    )

    @pl.when(taken)
    def _():
        target[...] = got[...]

    @pl.when(jnp.logical_not(taken))
    def _():
        target[...] = kept[...]


def merge_kernel(takers, column_count, row_count, kept_ref, got_ref, *refs):
    merge_into(takers, column_count, row_count, kept_ref, got_ref, refs[-1])


def column_kernel(
    takers, coef_ref, turned_ref, base_ref, factor_ref, *refs,
):
    row_count, column_count, domain, pao, lanes = coef_ref.shape
    held, got = refs[:column_count], refs[column_count : 2 * column_count]
    out_hbm, packed_ref, metric_ref, wide_ref, flat_ref, out_ref, sems = refs[2 * column_count :]
    npno = lanes // 2
    chunks = npno // 2
    for j in range(column_count):
        target = packed_ref.at[pl.ds(j * domain, domain)]
        merge_into(takers, column_count, row_count, held[j], got[j], target)
    slots = column_count * domain
    lows = [unpack(packed_ref[index], metric_ref.at[index]) for index in range(slots)]
    products = []
    for j in range(column_count):
        parts = []
        for s in range(domain):
            left = turned_ref[j, s]
            part = dot(left, metric_ref[j * domain + s]) + left.astype(F32) * lows[j * domain + s]
            parts.append(part.astype(BF16))
        products.append(jnp.concatenate(parts, axis=1))
    lane = lax.broadcasted_iota(jnp.int32, (chunks, lanes), 1)
    for i in range(row_count):
        for j in range(column_count):
            wide_ref[i, j] = dot(
                products[j][i * npno : (i + 1) * npno], coef_ref[i, j].reshape(domain * pao, lanes)
            )
            even = wide_ref[i, j, pl.ds(0, chunks, 2), :]
            odd = wide_ref[i, j, pl.ds(1, chunks, 2), :]
            total = jnp.where(lane < npno, pltpu.roll(even, npno, 1), odd)
            flat_ref[i, j] = base_ref[i, j] + factor_ref[i, j] * total
        for q in range(chunks):
            out_ref[i, :, q * lanes : (q + 1) * lanes] = flat_ref[i, :, q, :]
        pltpu.make_async_copy(out_ref.at[i], out_hbm.at[i], sems.at[i]).start()
    for i in range(row_count):
        pltpu.make_async_copy(out_ref.at[i], out_hbm.at[i], sems.at[i]).wait()


def call(kernel, out_shape, in_specs, out_specs, scratch, name, flops, moved):
    return pl.pallas_call(
        kernel,
        out_shape=out_shape,
        in_specs=in_specs,
        out_specs=out_specs,
        scratch_shapes=scratch,
        compiler_params=pltpu.CompilerParams(vmem_limit_bytes=48 * 2**20),
        cost_estimate=pl.CostEstimate(flops=flops, bytes_accessed=moved, transcendentals=0),
        name=name,
    )


def neighbours(block, axis, other):
    size, rest = lax.axis_size(axis), lax.axis_size(other)
    even = lax.ppermute(block, axis, [(n, n ^ 1) for n in range(size)])
    pairs = [(n, n + 1) for n in range(1, size - 1, 2)]
    if axis == "row" and size == 2 * len(pairs) + 2 and all(a ^ b == 3 for a, b in pairs):
        return [even, lax.ppermute(block, axis, [(n, n ^ 3) for n in range(size)])]
    joint = pairs + [(b, a) for a, b in pairs]
    alone = [n for n in range(size) if n not in dict(joint)]
    route = [((m, a), (m, b)) for m in range(rest) for a, b in joint]
    route += [((m, a), (m ^ 1, a)) for m in range(rest) for a in alone]

    def place(m, n):
        return n * rest + m if axis == "row" else m * size + n

    return [even, lax.ppermute(block, ("row", "col"), [(place(*a), place(*b)) for a, b in route])]


def after(block, others):
    return call(
        pass_kernel,
        jax.ShapeDtypeStruct(block.shape, block.dtype),
        [VMEM] + [ANY] * len(others),
        VMEM,
        [],
        "after_others",
        0,
        0,
    )(block, *others)


def gather_metrics(packed, cores, units, first, second):
    order = ring_order(units)
    forward = [
        (order[n] * cores + k, order[(n + 1) % units] * cores + k)
        for n in range(units)
        for k in range(cores)
    ]
    backward = [(b, a) for a, b in forward]
    turns = [packed] + [None] * (units - 1)
    up = down = packed
    for step in range(1, units // 2 + 1):
        if step == 2 and first:
            up = after(up, first)
        up = lax.ppermute(up, "col", forward)
        if step == 2 and second:
            up = after(up, second)
        turns[step] = up
        if units - step > units // 2:
            down = lax.ppermute(down, "col", backward)
            turns[units - step] = down
    buffers = []
    for turn in turns:
        buffers.append(turn)
        for side in range(1, cores):
            swap = [
                (u * cores + k, u * cores + (k + side) % cores)
                for u in range(units)
                for k in range(cores)
            ]
            buffers.append(lax.ppermute(turn, "col", swap))
    return buffers


def spread(pieces, sources, column_count, row_count, first):
    rows, columns = lax.axis_size("row"), len(sources)
    bits = rows.bit_length() - 1
    assert rows == 1 << bits
    reached = [[0] for _ in range(bits)]
    for step in range(bits):
        pairs, takers = [], []
        for turn in range(bits):
            bit = 1 << ((turn + step) % bits)
            pairs += [
                (row * columns + c, (row ^ bit) * columns + c)
                for c in range(turn, columns, bits)
                for row in range(rows)
            ]
            takers.append([away ^ bit for away in reached[turn]])
            reached[turn] = reached[turn] + takers[turn]
        got = [lax.ppermute(piece, ("row", "col"), pairs) for piece in pieces]
        if step < bits - 1:
            pieces = [
                call(
                    functools.partial(merge_kernel, takers, column_count, row_count),
                    jax.ShapeDtypeStruct(piece.shape, piece.dtype),
                    [VMEM, VMEM] + [ANY] * len(others),
                    VMEM,
                    [],
                    "merge",
                    0,
                    0,
                )(piece, block, *others)
                for piece, block, others in zip(pieces, got, first)
            ]
    return pieces + got, takers


def on_device(
    fitting,
    coefficients,
    amplitudes,
    intersections,
    virtual_energy,
    occupied_energy,
    kept_count,
    orbital_atoms,
    fock_partner,
    fock_value,
):
    row_count, column_count = amplitudes.shape[:2]
    held, aux, pao = fitting.shape
    domain = orbital_atoms.shape[1]
    npno = virtual_energy.shape[2]
    terms = intersections.shape[2]
    columns = lax.axis_size("col")
    cores = row_count // column_count
    units = columns // cores
    scale = (2 * domain * aux) ** (-0.5)
    depth = pao + EXTRA
    half = pao // 2

    chunks = npno // 2
    lanes = 2 * npno
    atoms_table, fit, own_block, partner, value, occupied, virtual, coefs, inter, kept = [
        pltpu.with_memory_space_constraint(array, pltpu.HBM)
        for array in (
            orbital_atoms.T,
            fitting,
            amplitudes,
            fock_partner.T,
            fock_value.T,
            occupied_energy,
            virtual_energy,
            coefficients,
            intersections,
            kept_count.T,
        )
    ]
    packed, table, lines = call(
        pack_kernel,
        (
            jax.ShapeDtypeStruct((held, depth, half), BF16),
            jax.ShapeDtypeStruct(atoms_table.shape, jnp.int32),
            jax.ShapeDtypeStruct((row_count, column_count, chunks, lanes), BF16),
        ),
        [HBM] * 3,
        (VMEM,) * 3,
        [
            pltpu.VMEM(fitting.shape, BF16),
            pltpu.VMEM(amplitudes.shape, BF16),
            pltpu.VMEM((row_count, chunks, column_count, lanes), F32),
            pltpu.SemaphoreType.DMA((held,)),
            pltpu.SemaphoreType.DMA(()),
            pltpu.SemaphoreType.DMA(()),
        ],
        "pack_metric",
        2 * held * aux * pao * pao,
        fitting.size * 2,
    )(atoms_table, own_block, fit)
    row_halos = neighbours(lines, "row", "col")
    col_halos = neighbours(lines, "col", "row")
    shape = (row_count, column_count, domain, pao, lanes)
    own_coefficients, column_coefficients, own_turned, turned = call(
        prepare_kernel,
        (
            jax.ShapeDtypeStruct(shape, BF16),
            jax.ShapeDtypeStruct(shape, BF16),
            jax.ShapeDtypeStruct((row_count, domain, column_count * npno, pao), BF16),
            jax.ShapeDtypeStruct((column_count, domain, row_count * npno, pao), BF16),
        ),
        [HBM],
        (VMEM,) * 4,
        [pltpu.SemaphoreType.DMA((row_count,)), pltpu.SemaphoreType.DMA((row_count,))],
        "prepare",
        0,
        coefficients.size * 4,
    )(coefs)
    mats = jax.ShapeDtypeStruct((row_count, column_count, terms, npno, npno), BF16)
    flat = jax.ShapeDtypeStruct((row_count, column_count, chunks, lanes), F32)
    mats, turned_mats, factor = call(
        functools.partial(square_kernel, scale),
        (mats, mats, flat),
        [HBM] * 2,
        (VMEM,) * 3,
        [
            pltpu.VMEM(intersections.shape, BF16),
            pltpu.VMEM((column_count, chunks, terms, lanes), F32),
            pltpu.VMEM((column_count, terms, npno, lanes), F32),
            pltpu.SMEM(kept_count.shape[::-1], jnp.int32),
            pltpu.SemaphoreType.DMA((row_count,)),
            pltpu.SemaphoreType.DMA(()),
        ],
        "square",
        0,
        intersections.size * 4,
    )(kept, inter)
    buffers = gather_metrics(packed, cores, units, row_halos + [turned_mats], [own_turned])
    blocks = [lines] + row_halos + col_halos
    wanted = column_count * domain
    atoms = len(buffers) * held
    *pieces, metrics = call(
        functools.partial(select_kernel, cores, units),
        tuple(
            jax.ShapeDtypeStruct((n, depth, half), BF16) for n in [domain] * column_count + [atoms]
        ),
        [SMEM] + [VMEM] * len(buffers),
        (VMEM,) * (column_count + 1),
        [],
        "select_column_atoms",
        0,
        (wanted + 2 * atoms) * depth * half * 4,
    )(table, *buffers)
    exchange = call(
        functools.partial(row_kernel, cores, units, held, scale),
        jax.ShapeDtypeStruct((row_count, column_count, npno, npno), F32),
        [SMEM] + [VMEM] * 3,
        VMEM,
        [pltpu.VMEM((domain, pao, pao), BF16)],
        "row_exchange",
        2 * row_count * column_count * domain * pao * npno * (pao + npno),
        coefficients.size,
    )(table, own_coefficients, own_turned, metrics)

    sources = [c * column_count // row_count for c in range(columns)]
    first = [[]] * (column_count - 1) + [[exchange] + col_halos]
    pieces, takers = spread(pieces, sources, column_count, row_count, first)

    base = call(
        couple_kernel,
        flat,
        [HBM] * 4 + [VMEM] * (4 + len(blocks)),
        VMEM,
        [
            pltpu.VMEM((row_count * column_count, npno, lanes), F32),
            pltpu.VMEM((len(blocks) * row_count, column_count, npno, npno), BF16),
            pltpu.SMEM(fock_partner.shape[::-1], jnp.int32),
            pltpu.SMEM(fock_value.shape[::-1], F32),
            pltpu.SMEM(occupied_energy.shape, F32),
            pltpu.VMEM(virtual_energy.shape, F32),
            pltpu.SemaphoreType.DMA((4,)),
        ],
        "couple",
        4 * row_count * column_count * terms * npno**3,
        intersections.size * 4,
    )(partner, value, occupied, virtual, mats, turned_mats, factor, exchange, *blocks)

    return call(
        functools.partial(column_kernel, takers),
        jax.ShapeDtypeStruct(amplitudes.shape, F32),
        [VMEM] * (4 + len(pieces)),
        HBM,
        [
            pltpu.VMEM((wanted, depth, half), BF16),
            pltpu.VMEM((wanted, pao, pao), BF16),
            pltpu.VMEM((row_count, column_count, npno, lanes), F32),
            pltpu.VMEM((row_count, column_count, chunks, lanes), F32),
            pltpu.VMEM(amplitudes.shape, F32),
            pltpu.SemaphoreType.DMA((row_count,)),
        ],
        "column_exchange",
        2 * row_count * column_count * domain * pao * npno * (pao + npno),
        coefficients.size,
    )(column_coefficients, turned, base, factor, *pieces)


def solution(mesh):
    placed = (
        P(("row", "col"), None, None),
        P("row", "col", None, None, None),
        P("row", "col", None),
        P("row", "col", None, None),
        P("row", "col", None),
        P(),
        P("row", "col"),
        P(),
        P(),
        P(),
    )
    return jax.shard_map(
        on_device, mesh=mesh, in_specs=placed, out_specs=P("row", "col", None), check_vma=False
    )
```

```python
import functools

import jax
import jax.numpy as jnp
from jax import lax
from jax.experimental import pallas as pl
from jax.experimental.pallas import tpu as pltpu
from jax.sharding import PartitionSpec as P

F32 = jnp.float32
BF16 = jnp.bfloat16
EXTRA = 16
VMEM = pl.BlockSpec(memory_space=pltpu.VMEM)
SMEM = pl.BlockSpec(memory_space=pltpu.SMEM)
HBM = pl.BlockSpec(memory_space=pltpu.HBM)
ANY = pl.BlockSpec(memory_space=pl.ANY)


def dot(a, b):
    return jnp.dot(a, b, preferred_element_type=F32)


def dot_nt(a, b):
    return lax.dot_general(a, b, (((1,), (1,)), ((), ())), preferred_element_type=F32)


def square_iota(n):
    return (
        lax.broadcasted_iota(jnp.int32, (n, n), 0),
        lax.broadcasted_iota(jnp.int32, (n, n), 1),
    )


def pack_kernel(
    atoms_ref, block_hbm, fit_ref, out_ref, table_ref, lines_ref,
    fits_ref, block_ref, flat_ref, sems, table_sem, block_sem,
):
    held = fit_ref.shape[0]
    half = fit_ref.shape[2] // 2
    row, col = square_iota(half)
    place = lax.broadcasted_iota(jnp.int32, (EXTRA, half), 0)
    fetches = [
        pltpu.make_async_copy(fit_ref.at[atom], fits_ref.at[atom], sems.at[atom])
        for atom in range(held)
    ]
    block = pltpu.make_async_copy(block_hbm, block_ref, block_sem)
    block.start()
    for fetch in fetches:
        fetch.start()
    table = pltpu.make_async_copy(atoms_ref, table_ref, table_sem)
    table.start()
    block.wait()
    row_count, column_count, chunks, lanes = lines_ref.shape
    for i in range(row_count):
        for q in range(chunks):
            flat_ref[i, q] = block_ref[i, :, q * lanes : (q + 1) * lanes].astype(F32)
    for i in range(row_count):
        for j in range(column_count):
            lines_ref[i, j] = flat_ref[i, :, j, :].astype(BF16)
    for fetch in fetches:
        fetch.wait()
    for atom in range(held):
        fit = fits_ref[atom]
        metric = lax.dot_general(fit, fit, (((0,), (0,)), ((), ())), preferred_element_type=F32)
        first, second = metric[:half, :half], metric[half:, half:]
        out_ref[atom, :half] = metric[:half, half:].astype(BF16)
        out_ref[atom, half : 2 * half] = jnp.where(row <= col, first, second).astype(BF16)
        lines = [jnp.sum(jnp.where(row == col, m, 0.0), axis=0, keepdims=True) for m in (first, second)]
        high = [line.astype(BF16).astype(F32) for line in lines]
        extra = jnp.where(
            place == 0,
            high[1],
            jnp.where(
                place == 1,
                lines[0] - high[0],
                jnp.where(place == 2, lines[1] - high[1], 0.0),
            ),
        )
        out_ref[atom, 2 * half :] = extra.astype(BF16)
    table.wait()


def unpack(packed, metric_ref):
    half = packed.shape[1]
    row, col = square_iota(half)
    corner = packed[:half]
    both = packed[half : 2 * half].astype(F32)
    extra = packed[2 * half :].astype(F32)
    turned = both.T
    metric_ref[:half, :half] = jnp.where(row <= col, both, turned).astype(BF16)
    metric_ref[:half, half:] = corner
    metric_ref[half:, :half] = corner.astype(F32).T.astype(BF16)
    metric_ref[half:, half:] = jnp.where(
        row > col, both, jnp.where(row == col, extra[0:1], turned)
    ).astype(BF16)
    return jnp.concatenate([extra[1:2], extra[2:3]], axis=1)


def ring_order(units):
    return [0] + list(range(1, units, 2)) + list(range(units - units % 2 - (0 if units % 2 else 2), 0, -2))


def ring_place(unit, units):
    return jnp.where(unit % 2 == 1, (unit + 1) // 2, (units - unit // 2) % units)


def pick_place(atom, row_place, col_place, cores, units, held):
    label = jnp.clip(atom - row_place * (units * cores * held), 0, units * cores * held - 1)
    owner, slot = label // held, label % held
    turn = (ring_place(col_place // cores, units) - ring_place(owner // cores, units) + units) % units
    side = (col_place % cores - owner % cores + cores) % cores
    return (turn * cores + side) * held + slot


def select_kernel(cores, units, atoms_ref, *refs):
    count = units * cores
    buffers, pieces, all_ref = refs[:count], refs[count:-1], refs[-1]
    held = buffers[0].shape[0]
    row_place, col_place = lax.axis_index("row"), lax.axis_index("col")
    for index, buffer in enumerate(buffers):
        all_ref[index * held : (index + 1) * held] = buffer[...]
    for j, piece_ref in enumerate(pieces):
        for s in range(piece_ref.shape[0]):
            atom = atoms_ref[s, col_place * len(pieces) + j]
            place = pick_place(atom, row_place, col_place, cores, units, held)
            piece_ref[s] = all_ref[place]


def pass_kernel(block_ref, *refs):
    refs[-1][...] = block_ref[...]


def neighbour_place(place, turn):
    return jnp.where(turn == 0, 0, jnp.where((place + turn) == jnp.bitwise_xor(place, 1), 1, 2))


def couple_kernel(
    partner_hbm, value_hbm, occupied_hbm, virtual_hbm, inter_ref, turned_ref, factor_ref, *refs,
):
    exchange_ref, blocks = refs[0], refs[1:6]
    base_ref, wide_ref, mats_ref = refs[6:9]
    partner_ref, value_ref, occupied_ref, virtual_ref, sems = refs[9:]
    row_count, column_count, terms, npno, _ = inter_ref.shape
    chunks, lanes = base_ref.shape[2:]
    partners = terms // 2
    row_place, col_place = lax.axis_index("row"), lax.axis_index("col")
    first_row = row_place * row_count
    first_col = col_place * column_count
    fetches = [
        pltpu.make_async_copy(source, target, sems.at[n])
        for n, (source, target) in enumerate(
            [
                (partner_hbm, partner_ref),
                (value_hbm, value_ref),
                (occupied_hbm, occupied_ref),
                (virtual_hbm, virtual_ref),
            ]
        )
    ]
    for fetch in fetches:
        fetch.start()

    for index, block in enumerate(blocks):
        for i in range(row_count):
            for j in range(column_count):
                lines = block[i, j].astype(F32)
                wide = wide_ref.at[(i * column_count + j) % wide_ref.shape[0]]
                wide[pl.ds(0, chunks, 2), :] = lines
                wide[pl.ds(1, chunks, 2), :] = pltpu.roll(lines, npno, 1)
                mats_ref[index * row_count + i, j] = wide[:, :npno].astype(BF16)
    for fetch in fetches:
        fetch.wait()
    lane = lax.broadcasted_iota(jnp.int32, (chunks, lanes), 1)

    def one_row(i, carry):
        for j in range(column_count):
            total = jnp.zeros((npno, npno), F32)
            for n in range(terms):
                if n < partners:
                    away = partner_ref[n, first_row + i] - first_row + row_count
                    turn = away // row_count - 1
                    index = neighbour_place(row_place, turn) * row_count + away % row_count
                    weight = value_ref[n, first_row + i]
                    partner = mats_ref[index, j]
                else:
                    away = partner_ref[n - partners, first_col + j] - first_col + column_count
                    turn = away // column_count - 1
                    index = neighbour_place(col_place, turn)
                    index = jnp.where(index == 0, 0, index + 2) * row_count + i
                    weight = value_ref[n - partners, first_col + j]
                    partner = mats_ref[index, away % column_count]
                half = dot(inter_ref[i, j, n], partner).astype(BF16)
                total = total + weight * dot(half, turned_ref[i, j, n])
            levels = jnp.broadcast_to(virtual_ref[i, pl.ds(j, 1)], (npno, npno))
            shift = levels + levels.T - occupied_ref[first_row + i] - occupied_ref[first_col + j]
            wide = wide_ref.at[j]
            wide[:, :npno] = exchange_ref[i, j] + shift * mats_ref[i, j].astype(F32) - total
            even = wide[pl.ds(0, chunks, 2), :]
            odd = pltpu.roll(wide[pl.ds(1, chunks, 2), :], npno, 1)
            result = jnp.where(lane < npno, even, odd)
            base_ref[i, j] = jnp.where(factor_ref[i, j] == 0.0, 0.0, result)
        return carry

    lax.fori_loop(0, row_count, one_row, 0)


def prepare_kernel(coef_hbm, own_ref, coef_ref, own_turned_ref, turned_ref, own_sems, coef_sems):
    row_count, column_count, domain, _, lanes = own_ref.shape
    npno = lanes // 2

    def fetch(i, first, target_ref, sems):
        return pltpu.make_async_copy(
            coef_hbm.at[i, :, pl.ds(first, domain)], target_ref.at[i], sems.at[i]
        )

    for i in range(row_count):
        fetch(i, 0, own_ref, own_sems).start()
        fetch(i, domain, coef_ref, coef_sems).start()
    for i in range(row_count):
        fetch(i, 0, own_ref, own_sems).wait()
        for j in range(column_count):
            for s in range(domain):
                own_turned_ref[i, s, j * npno : (j + 1) * npno] = own_ref[i, j, s].T[:npno]
        fetch(i, domain, coef_ref, coef_sems).wait()
        for j in range(column_count):
            for s in range(domain):
                turned_ref[j, s, i * npno : (i + 1) * npno] = coef_ref[i, j, s].T[:npno]


def square_kernel(
    scale, kept_hbm, inter_hbm, mats_ref, turned_mats_ref, factor_ref,
    inter_ref, flat_ref, wide_ref, kept_ref, inter_sems, kept_sem,
):
    row_count, column_count, terms, npno, _ = mats_ref.shape
    chunks, lanes = factor_ref.shape[2:]

    def fetch_inter(i):
        return pltpu.make_async_copy(inter_hbm.at[i], inter_ref.at[i], inter_sems.at[i])

    kept_copy = pltpu.make_async_copy(kept_hbm, kept_ref, kept_sem)
    kept_copy.start()
    for i in range(row_count):
        fetch_inter(i).start()

    def one_row(i, carry):
        fetch_inter(i).wait()
        for j in range(column_count):
            for q in range(chunks):
                flat_ref[j, q] = inter_ref[i, j, :, q * lanes : (q + 1) * lanes].astype(F32)
            for n in range(terms):
                lines = flat_ref[j, :, n, :]
                wide_ref[j, n, pl.ds(0, chunks, 2), :] = lines
                wide_ref[j, n, pl.ds(1, chunks, 2), :] = pltpu.roll(lines, npno, 1)
        for j in range(column_count):
            for n in range(terms):
                inter = wide_ref[j, n, :, :npno]
                mats_ref[i, j, n] = inter.astype(BF16)
                turned_mats_ref[i, j, n] = inter.T.astype(BF16)
        return carry

    lax.fori_loop(0, row_count, one_row, 0)
    kept_copy.wait()
    place = lax.broadcasted_iota(jnp.int32, (chunks, lanes), 0)
    lane = lax.broadcasted_iota(jnp.int32, (chunks, lanes), 1)
    first = 2 * place + jnp.where(lane < npno, 0, 1)
    second = jnp.where(lane < npno, lane, lane - npno)
    most = jnp.maximum(first, second)
    for i in range(row_count):
        for j in range(column_count):
            factor_ref[i, j] = jnp.where(most < kept_ref[j, i], scale, 0.0)


def row_kernel(cores, units, held, scale, atoms_ref, coef_ref, turned_ref, all_ref, out_ref, metric_ref):
    row_count, column_count, domain, pao, lanes = coef_ref.shape
    npno = lanes // 2
    row_place, col_place = lax.axis_index("row"), lax.axis_index("col")
    lows = []
    for i in range(row_count):
        for s in range(domain):
            atom = atoms_ref[s, row_place * row_count + i]
            place = pick_place(atom, row_place, col_place, cores, units, held)
            lows.append(unpack(all_ref[place], metric_ref.at[i * domain + s]))
    for i in range(row_count):
        parts = []
        for s in range(domain):
            left = turned_ref[i, s]
            part = dot(left, metric_ref[i * domain + s]) + left.astype(F32) * lows[i * domain + s]
            parts.append(part.astype(BF16))
        product = jnp.concatenate(parts, axis=1)
        for j in range(column_count):
            total = dot(
                product[j * npno : (j + 1) * npno], coef_ref[i, j].reshape(domain * pao, lanes)
            )
            out_ref[i, j] = total[:, npno:] * scale


def merge_into(takers, column_count, row_count, kept, got, target):
    col_place = lax.axis_index("col")
    away = jnp.bitwise_xor(lax.axis_index("row"), col_place * column_count // row_count)
    turn = col_place % len(takers)
    taken = functools.reduce(
        jnp.logical_or,
        [(turn == n) & (away == taker) for n, these in enumerate(takers) for taker in these],
    )

    @pl.when(taken)
    def _():
        target[...] = got[...]

    @pl.when(jnp.logical_not(taken))
    def _():
        target[...] = kept[...]


def merge_kernel(takers, column_count, row_count, kept_ref, got_ref, *refs):
    merge_into(takers, column_count, row_count, kept_ref, got_ref, refs[-1])


def column_kernel(
    takers, coef_ref, turned_ref, base_ref, factor_ref, *refs,
):
    row_count, column_count, domain, pao, lanes = coef_ref.shape
    held, got = refs[:column_count], refs[column_count : 2 * column_count]
    out_hbm, packed_ref, metric_ref, wide_ref, flat_ref, out_ref, sems = refs[2 * column_count :]
    npno = lanes // 2
    chunks = npno // 2
    for j in range(column_count):
        target = packed_ref.at[pl.ds(j * domain, domain)]
        merge_into(takers, column_count, row_count, held[j], got[j], target)
    slots = column_count * domain
    lows = [unpack(packed_ref[index], metric_ref.at[index]) for index in range(slots)]
    products = []
    for j in range(column_count):
        parts = []
        for s in range(domain):
            left = turned_ref[j, s]
            part = dot(left, metric_ref[j * domain + s]) + left.astype(F32) * lows[j * domain + s]
            parts.append(part.astype(BF16))
        products.append(jnp.concatenate(parts, axis=1))
    lane = lax.broadcasted_iota(jnp.int32, (chunks, lanes), 1)
    for i in range(row_count):
        for j in range(column_count):
            wide_ref[i, j] = dot(
                products[j][i * npno : (i + 1) * npno], coef_ref[i, j].reshape(domain * pao, lanes)
            )
            even = wide_ref[i, j, pl.ds(0, chunks, 2), :]
            odd = wide_ref[i, j, pl.ds(1, chunks, 2), :]
            total = jnp.where(lane < npno, pltpu.roll(even, npno, 1), odd)
            flat_ref[i, j] = base_ref[i, j] + factor_ref[i, j] * total
        for q in range(chunks):
            out_ref[i, :, q * lanes : (q + 1) * lanes] = flat_ref[i, :, q, :]
        pltpu.make_async_copy(out_ref.at[i], out_hbm.at[i], sems.at[i]).start()
    for i in range(row_count):
        pltpu.make_async_copy(out_ref.at[i], out_hbm.at[i], sems.at[i]).wait()


def call(kernel, out_shape, in_specs, out_specs, scratch, name, flops, moved):
    return pl.pallas_call(
        kernel,
        out_shape=out_shape,
        in_specs=in_specs,
        out_specs=out_specs,
        scratch_shapes=scratch,
        compiler_params=pltpu.CompilerParams(vmem_limit_bytes=48 * 2**20),
        cost_estimate=pl.CostEstimate(flops=flops, bytes_accessed=moved, transcendentals=0),
        name=name,
    )


def neighbours(block, axis, other):
    size, rest = lax.axis_size(axis), lax.axis_size(other)
    even = lax.ppermute(block, axis, [(n, n ^ 1) for n in range(size)])
    pairs = [(n, n + 1) for n in range(1, size - 1, 2)]
    if axis == "row" and size == 2 * len(pairs) + 2 and all(a ^ b == 3 for a, b in pairs):
        return [even, lax.ppermute(block, axis, [(n, n ^ 3) for n in range(size)])]
    joint = pairs + [(b, a) for a, b in pairs]
    alone = [n for n in range(size) if n not in dict(joint)]
    route = [((m, a), (m, b)) for m in range(rest) for a, b in joint]
    trade = 1 if rest % 4 else 2
    route += [((m, a), (m ^ trade, a)) for m in range(rest) for a in alone]

    def place(m, n):
        return n * rest + m if axis == "row" else m * size + n

    return [even, lax.ppermute(block, ("row", "col"), [(place(*a), place(*b)) for a, b in route])]


def after(block, others):
    return call(
        pass_kernel,
        jax.ShapeDtypeStruct(block.shape, block.dtype),
        [VMEM] + [ANY] * len(others),
        VMEM,
        [],
        "after_others",
        0,
        0,
    )(block, *others)


def gather_metrics(packed, cores, units, first, second):
    order = ring_order(units)
    forward = [
        (order[n] * cores + k, order[(n + 1) % units] * cores + k)
        for n in range(units)
        for k in range(cores)
    ]
    backward = [(b, a) for a, b in forward]
    turns = [packed] + [None] * (units - 1)
    up = down = packed
    for step in range(1, units // 2 + 1):
        if step == 2 and first:
            up = after(up, first)
        up = lax.ppermute(up, "col", forward)
        if step == 2 and second:
            up = after(up, second)
        turns[step] = up
        if units - step > units // 2:
            down = lax.ppermute(down, "col", backward)
            turns[units - step] = down
    buffers = []
    for turn in turns:
        buffers.append(turn)
        for side in range(1, cores):
            swap = [
                (u * cores + k, u * cores + (k + side) % cores)
                for u in range(units)
                for k in range(cores)
            ]
            buffers.append(lax.ppermute(turn, "col", swap))
    return buffers


def spread(pieces, sources, column_count, row_count, first):
    rows, columns = lax.axis_size("row"), len(sources)
    bits = rows.bit_length() - 1
    assert rows == 1 << bits
    reached = [[0] for _ in range(bits)]
    for step in range(bits):
        pairs, takers = [], []
        for turn in range(bits):
            bit = 1 << ((turn + step) % bits)
            pairs += [
                (row * columns + c, (row ^ bit) * columns + c)
                for c in range(turn, columns, bits)
                for row in range(rows)
            ]
            takers.append([away ^ bit for away in reached[turn]])
            reached[turn] = reached[turn] + takers[turn]
        got = [lax.ppermute(piece, ("row", "col"), pairs) for piece in pieces]
        if step < bits - 1:
            pieces = [
                call(
                    functools.partial(merge_kernel, takers, column_count, row_count),
                    jax.ShapeDtypeStruct(piece.shape, piece.dtype),
                    [VMEM, VMEM] + [ANY] * len(others),
                    VMEM,
                    [],
                    "merge",
                    0,
                    0,
                )(piece, block, *others)
                for piece, block, others in zip(pieces, got, first)
            ]
    return pieces + got, takers


def on_device(
    fitting,
    coefficients,
    amplitudes,
    intersections,
    virtual_energy,
    occupied_energy,
    kept_count,
    orbital_atoms,
    fock_partner,
    fock_value,
):
    row_count, column_count = amplitudes.shape[:2]
    held, aux, pao = fitting.shape
    domain = orbital_atoms.shape[1]
    npno = virtual_energy.shape[2]
    terms = intersections.shape[2]
    columns = lax.axis_size("col")
    cores = row_count // column_count
    units = columns // cores
    scale = (2 * domain * aux) ** (-0.5)
    depth = pao + EXTRA
    half = pao // 2

    chunks = npno // 2
    lanes = 2 * npno
    atoms_table, fit, own_block, partner, value, occupied, virtual, coefs, inter, kept = [
        pltpu.with_memory_space_constraint(array, pltpu.HBM)
        for array in (
            orbital_atoms.T,
            fitting,
            amplitudes,
            fock_partner.T,
            fock_value.T,
            occupied_energy,
            virtual_energy,
            coefficients,
            intersections,
            kept_count.T,
        )
    ]
    packed, table, lines = call(
        pack_kernel,
        (
            jax.ShapeDtypeStruct((held, depth, half), BF16),
            jax.ShapeDtypeStruct(atoms_table.shape, jnp.int32),
            jax.ShapeDtypeStruct((row_count, column_count, chunks, lanes), BF16),
        ),
        [HBM] * 3,
        (VMEM,) * 3,
        [
            pltpu.VMEM(fitting.shape, BF16),
            pltpu.VMEM(amplitudes.shape, BF16),
            pltpu.VMEM((row_count, chunks, column_count, lanes), F32),
            pltpu.SemaphoreType.DMA((held,)),
            pltpu.SemaphoreType.DMA(()),
            pltpu.SemaphoreType.DMA(()),
        ],
        "pack_metric",
        2 * held * aux * pao * pao,
        fitting.size * 2,
    )(atoms_table, own_block, fit)
    row_halos = neighbours(lines, "row", "col")
    col_halos = neighbours(lines, "col", "row")
    shape = (row_count, column_count, domain, pao, lanes)
    own_coefficients, column_coefficients, own_turned, turned = call(
        prepare_kernel,
        (
            jax.ShapeDtypeStruct(shape, BF16),
            jax.ShapeDtypeStruct(shape, BF16),
            jax.ShapeDtypeStruct((row_count, domain, column_count * npno, pao), BF16),
            jax.ShapeDtypeStruct((column_count, domain, row_count * npno, pao), BF16),
        ),
        [HBM],
        (VMEM,) * 4,
        [pltpu.SemaphoreType.DMA((row_count,)), pltpu.SemaphoreType.DMA((row_count,))],
        "prepare",
        0,
        coefficients.size * 4,
    )(coefs)
    mats = jax.ShapeDtypeStruct((row_count, column_count, terms, npno, npno), BF16)
    flat = jax.ShapeDtypeStruct((row_count, column_count, chunks, lanes), F32)
    mats, turned_mats, factor = call(
        functools.partial(square_kernel, scale),
        (mats, mats, flat),
        [HBM] * 2,
        (VMEM,) * 3,
        [
            pltpu.VMEM(intersections.shape, BF16),
            pltpu.VMEM((column_count, chunks, terms, lanes), F32),
            pltpu.VMEM((column_count, terms, npno, lanes), F32),
            pltpu.SMEM(kept_count.shape[::-1], jnp.int32),
            pltpu.SemaphoreType.DMA((row_count,)),
            pltpu.SemaphoreType.DMA(()),
        ],
        "square",
        0,
        intersections.size * 4,
    )(kept, inter)
    buffers = gather_metrics(packed, cores, units, row_halos + [turned_mats], [own_turned])
    blocks = [lines] + row_halos + col_halos
    wanted = column_count * domain
    atoms = len(buffers) * held
    *pieces, metrics = call(
        functools.partial(select_kernel, cores, units),
        tuple(
            jax.ShapeDtypeStruct((n, depth, half), BF16) for n in [domain] * column_count + [atoms]
        ),
        [SMEM] + [VMEM] * len(buffers),
        (VMEM,) * (column_count + 1),
        [],
        "select_column_atoms",
        0,
        (wanted + 2 * atoms) * depth * half * 4,
    )(table, *buffers)
    exchange = call(
        functools.partial(row_kernel, cores, units, held, scale),
        jax.ShapeDtypeStruct((row_count, column_count, npno, npno), F32),
        [SMEM] + [VMEM] * 3,
        VMEM,
        [pltpu.VMEM((row_count * domain, pao, pao), BF16)],
        "row_exchange",
        2 * row_count * column_count * domain * pao * npno * (pao + npno),
        coefficients.size,
    )(table, own_coefficients, own_turned, metrics)

    sources = [c * column_count // row_count for c in range(columns)]
    first = [[]] * (column_count - 1) + [[exchange] + col_halos]
    pieces, takers = spread(pieces, sources, column_count, row_count, first)

    base = call(
        couple_kernel,
        flat,
        [HBM] * 4 + [VMEM] * (4 + len(blocks)),
        VMEM,
        [
            pltpu.VMEM((row_count * column_count, npno, lanes), F32),
            pltpu.VMEM((len(blocks) * row_count, column_count, npno, npno), BF16),
            pltpu.SMEM(fock_partner.shape[::-1], jnp.int32),
            pltpu.SMEM(fock_value.shape[::-1], F32),
            pltpu.SMEM(occupied_energy.shape, F32),
            pltpu.VMEM(virtual_energy.shape, F32),
            pltpu.SemaphoreType.DMA((4,)),
        ],
        "couple",
        4 * row_count * column_count * terms * npno**3,
        intersections.size * 4,
    )(partner, value, occupied, virtual, mats, turned_mats, factor, exchange, *blocks)

    return call(
        functools.partial(column_kernel, takers),
        jax.ShapeDtypeStruct(amplitudes.shape, F32),
        [VMEM] * (4 + len(pieces)),
        HBM,
        [
            pltpu.VMEM((wanted, depth, half), BF16),
            pltpu.VMEM((wanted, pao, pao), BF16),
            pltpu.VMEM((row_count, column_count, npno, lanes), F32),
            pltpu.VMEM((row_count, column_count, chunks, lanes), F32),
            pltpu.VMEM(amplitudes.shape, F32),
            pltpu.SemaphoreType.DMA((row_count,)),
        ],
        "column_exchange",
        2 * row_count * column_count * domain * pao * npno * (pao + npno),
        coefficients.size,
    )(column_coefficients, turned, base, factor, *pieces)


def solution(mesh):
    placed = (
        P(("row", "col"), None, None),
        P("row", "col", None, None, None),
        P("row", "col", None),
        P("row", "col", None, None),
        P("row", "col", None),
        P(),
        P("row", "col"),
        P(),
        P(),
        P(),
    )
    return jax.shard_map(
        on_device, mesh=mesh, in_specs=placed, out_specs=P("row", "col", None), check_vma=False
    )
```

```python
import functools

import jax
import jax.numpy as jnp
from jax import lax
from jax.experimental import pallas as pl
from jax.experimental.pallas import tpu as pltpu
from jax.sharding import PartitionSpec as P

F32 = jnp.float32
BF16 = jnp.bfloat16
EXTRA = 16
VMEM = pl.BlockSpec(memory_space=pltpu.VMEM)
SMEM = pl.BlockSpec(memory_space=pltpu.SMEM)
HBM = pl.BlockSpec(memory_space=pltpu.HBM)
ANY = pl.BlockSpec(memory_space=pl.ANY)


def dot(a, b):
    return jnp.dot(a, b, preferred_element_type=F32)


def dot_nt(a, b):
    return lax.dot_general(a, b, (((1,), (1,)), ((), ())), preferred_element_type=F32)


def square_iota(n):
    return (
        lax.broadcasted_iota(jnp.int32, (n, n), 0),
        lax.broadcasted_iota(jnp.int32, (n, n), 1),
    )


def pack_kernel(
    atoms_ref, block_hbm, fit_ref, out_ref, table_ref, lines_ref,
    fits_ref, block_ref, flat_ref, sems, table_sem, block_sem,
):
    held = fit_ref.shape[0]
    half = fit_ref.shape[2] // 2
    row, col = square_iota(half)
    place = lax.broadcasted_iota(jnp.int32, (EXTRA, half), 0)
    fetches = [
        pltpu.make_async_copy(fit_ref.at[atom], fits_ref.at[atom], sems.at[atom])
        for atom in range(held)
    ]
    block = pltpu.make_async_copy(block_hbm, block_ref, block_sem)
    block.start()
    for fetch in fetches:
        fetch.start()
    table = pltpu.make_async_copy(atoms_ref, table_ref, table_sem)
    table.start()
    block.wait()
    row_count, column_count, chunks, lanes = lines_ref.shape
    for i in range(row_count):
        for q in range(chunks):
            flat_ref[i, q] = block_ref[i, :, q * lanes : (q + 1) * lanes].astype(F32)
    for i in range(row_count):
        for j in range(column_count):
            lines_ref[i, j] = flat_ref[i, :, j, :].astype(BF16)
    for fetch in fetches:
        fetch.wait()
    for atom in range(held):
        fit = fits_ref[atom]
        metric = lax.dot_general(fit, fit, (((0,), (0,)), ((), ())), preferred_element_type=F32)
        first, second = metric[:half, :half], metric[half:, half:]
        out_ref[atom, :half] = metric[:half, half:].astype(BF16)
        out_ref[atom, half : 2 * half] = jnp.where(row <= col, first, second).astype(BF16)
        lines = [jnp.sum(jnp.where(row == col, m, 0.0), axis=0, keepdims=True) for m in (first, second)]
        high = [line.astype(BF16).astype(F32) for line in lines]
        extra = jnp.where(
            place == 0,
            high[1],
            jnp.where(
                place == 1,
                lines[0] - high[0],
                jnp.where(place == 2, lines[1] - high[1], 0.0),
            ),
        )
        out_ref[atom, 2 * half :] = extra.astype(BF16)
    table.wait()


def unpack(packed, metric_ref):
    half = packed.shape[1]
    row, col = square_iota(half)
    corner = packed[:half]
    both = packed[half : 2 * half].astype(F32)
    extra = packed[2 * half :].astype(F32)
    turned = both.T
    metric_ref[:half, :half] = jnp.where(row <= col, both, turned).astype(BF16)
    metric_ref[:half, half:] = corner
    metric_ref[half:, :half] = corner.astype(F32).T.astype(BF16)
    metric_ref[half:, half:] = jnp.where(
        row > col, both, jnp.where(row == col, extra[0:1], turned)
    ).astype(BF16)
    return jnp.concatenate([extra[1:2], extra[2:3]], axis=1)


def ring_order(units):
    return [0] + list(range(1, units, 2)) + list(range(units - units % 2 - (0 if units % 2 else 2), 0, -2))


def ring_place(unit, units):
    return jnp.where(unit % 2 == 1, (unit + 1) // 2, (units - unit // 2) % units)


def pick_place(atom, row_place, col_place, cores, units, held):
    label = jnp.clip(atom - row_place * (units * cores * held), 0, units * cores * held - 1)
    owner, slot = label // held, label % held
    turn = (ring_place(col_place // cores, units) - ring_place(owner // cores, units) + units) % units
    side = (col_place % cores - owner % cores + cores) % cores
    return (turn * cores + side) * held + slot


def select_kernel(cores, units, atoms_ref, *refs):
    count = units * cores
    buffers, pieces, all_ref = refs[:count], refs[count:-1], refs[-1]
    held = buffers[0].shape[0]
    row_place, col_place = lax.axis_index("row"), lax.axis_index("col")
    for index, buffer in enumerate(buffers):
        all_ref[index * held : (index + 1) * held] = buffer[...]
    for j, piece_ref in enumerate(pieces):
        for s in range(piece_ref.shape[0]):
            atom = atoms_ref[s, col_place * len(pieces) + j]
            place = pick_place(atom, row_place, col_place, cores, units, held)
            piece_ref[s] = all_ref[place]


def pass_kernel(block_ref, *refs):
    refs[-1][...] = block_ref[...]


def neighbour_place(place, turn):
    return jnp.where(turn == 0, 0, jnp.where((place + turn) == jnp.bitwise_xor(place, 1), 1, 2))


def couple_kernel(
    partner_hbm, value_hbm, occupied_hbm, virtual_hbm, inter_ref, turned_ref, factor_ref, *refs,
):
    exchange_ref, blocks = refs[0], refs[1:6]
    base_ref, wide_ref, mats_ref = refs[6:9]
    partner_ref, value_ref, occupied_ref, virtual_ref, sems = refs[9:]
    row_count, column_count, terms, npno, _ = inter_ref.shape
    chunks, lanes = base_ref.shape[2:]
    partners = terms // 2
    row_place, col_place = lax.axis_index("row"), lax.axis_index("col")
    first_row = row_place * row_count
    first_col = col_place * column_count
    fetches = [
        pltpu.make_async_copy(source, target, sems.at[n])
        for n, (source, target) in enumerate(
            [
                (partner_hbm, partner_ref),
                (value_hbm, value_ref),
                (occupied_hbm, occupied_ref),
                (virtual_hbm, virtual_ref),
            ]
        )
    ]
    for fetch in fetches:
        fetch.start()

    for index, block in enumerate(blocks):
        for i in range(row_count):
            for j in range(column_count):
                lines = block[i, j].astype(F32)
                wide = wide_ref.at[(i * column_count + j) % wide_ref.shape[0]]
                wide[pl.ds(0, chunks, 2), :] = lines
                wide[pl.ds(1, chunks, 2), :] = pltpu.roll(lines, npno, 1)
                mats_ref[index * row_count + i, j] = wide[:, :npno].astype(BF16)
    for fetch in fetches:
        fetch.wait()
    lane = lax.broadcasted_iota(jnp.int32, (chunks, lanes), 1)

    def one_row(i, carry):
        for j in range(column_count):
            total = jnp.zeros((npno, npno), F32)
            for n in range(terms):
                if n < partners:
                    away = partner_ref[n, first_row + i] - first_row + row_count
                    turn = away // row_count - 1
                    index = neighbour_place(row_place, turn) * row_count + away % row_count
                    weight = value_ref[n, first_row + i]
                    partner = mats_ref[index, j]
                else:
                    away = partner_ref[n - partners, first_col + j] - first_col + column_count
                    turn = away // column_count - 1
                    index = neighbour_place(col_place, turn)
                    index = jnp.where(index == 0, 0, index + 2) * row_count + i
                    weight = value_ref[n - partners, first_col + j]
                    partner = mats_ref[index, away % column_count]
                half = dot(inter_ref[i, j, n], partner).astype(BF16)
                total = total + weight * dot(half, turned_ref[i, j, n])
            levels = jnp.broadcast_to(virtual_ref[i, pl.ds(j, 1)], (npno, npno))
            shift = levels + levels.T - occupied_ref[first_row + i] - occupied_ref[first_col + j]
            wide = wide_ref.at[j]
            wide[:, :npno] = exchange_ref[i, j] + shift * mats_ref[i, j].astype(F32) - total
            even = wide[pl.ds(0, chunks, 2), :]
            odd = pltpu.roll(wide[pl.ds(1, chunks, 2), :], npno, 1)
            result = jnp.where(lane < npno, even, odd)
            base_ref[i, j] = jnp.where(factor_ref[i, j] == 0.0, 0.0, result)
        return carry

    lax.fori_loop(0, row_count, one_row, 0)


def prepare_kernel(coef_hbm, own_ref, coef_ref, own_turned_ref, turned_ref, own_sems, coef_sems):
    row_count, column_count, domain, _, lanes = own_ref.shape
    npno = lanes // 2

    def fetch(i, first, target_ref, sems):
        return pltpu.make_async_copy(
            coef_hbm.at[i, :, pl.ds(first, domain)], target_ref.at[i], sems.at[i]
        )

    for i in range(row_count):
        fetch(i, 0, own_ref, own_sems).start()
        fetch(i, domain, coef_ref, coef_sems).start()
    for i in range(row_count):
        fetch(i, 0, own_ref, own_sems).wait()
        for j in range(column_count):
            for s in range(domain):
                own_turned_ref[i, s, j * npno : (j + 1) * npno] = own_ref[i, j, s].T[:npno]
        fetch(i, domain, coef_ref, coef_sems).wait()
        for j in range(column_count):
            for s in range(domain):
                turned_ref[j, s, i * npno : (i + 1) * npno] = coef_ref[i, j, s].T[:npno]


def square_kernel(
    scale, kept_hbm, inter_hbm, mats_ref, turned_mats_ref, factor_ref,
    inter_ref, flat_ref, wide_ref, kept_ref, inter_sems, kept_sem,
):
    row_count, column_count, terms, npno, _ = mats_ref.shape
    chunks, lanes = factor_ref.shape[2:]

    def fetch_inter(i):
        return pltpu.make_async_copy(inter_hbm.at[i], inter_ref.at[i], inter_sems.at[i])

    kept_copy = pltpu.make_async_copy(kept_hbm, kept_ref, kept_sem)
    kept_copy.start()
    for i in range(row_count):
        fetch_inter(i).start()

    def one_row(i, carry):
        fetch_inter(i).wait()
        for j in range(column_count):
            for q in range(chunks):
                flat_ref[j, q] = inter_ref[i, j, :, q * lanes : (q + 1) * lanes].astype(F32)
            for n in range(terms):
                lines = flat_ref[j, :, n, :]
                wide_ref[j, n, pl.ds(0, chunks, 2), :] = lines
                wide_ref[j, n, pl.ds(1, chunks, 2), :] = pltpu.roll(lines, npno, 1)
        for j in range(column_count):
            for n in range(terms):
                inter = wide_ref[j, n, :, :npno]
                mats_ref[i, j, n] = inter.astype(BF16)
                turned_mats_ref[i, j, n] = inter.T.astype(BF16)
        return carry

    lax.fori_loop(0, row_count, one_row, 0)
    kept_copy.wait()
    place = lax.broadcasted_iota(jnp.int32, (chunks, lanes), 0)
    lane = lax.broadcasted_iota(jnp.int32, (chunks, lanes), 1)
    first = 2 * place + jnp.where(lane < npno, 0, 1)
    second = jnp.where(lane < npno, lane, lane - npno)
    most = jnp.maximum(first, second)
    for i in range(row_count):
        for j in range(column_count):
            factor_ref[i, j] = jnp.where(most < kept_ref[j, i], scale, 0.0)


def row_kernel(cores, units, held, scale, atoms_ref, coef_ref, turned_ref, all_ref, out_ref, metric_ref):
    row_count, column_count, domain, pao, lanes = coef_ref.shape
    npno = lanes // 2
    row_place, col_place = lax.axis_index("row"), lax.axis_index("col")
    lows = []
    for i in range(row_count):
        for s in range(domain):
            atom = atoms_ref[s, row_place * row_count + i]
            place = pick_place(atom, row_place, col_place, cores, units, held)
            lows.append(unpack(all_ref[place], metric_ref.at[i * domain + s]))
    for i in range(row_count):
        parts = []
        for s in range(domain):
            left = turned_ref[i, s]
            part = dot(left, metric_ref[i * domain + s]) + left.astype(F32) * lows[i * domain + s]
            parts.append(part.astype(BF16))
        product = jnp.concatenate(parts, axis=1)
        for j in range(column_count):
            total = dot(
                product[j * npno : (j + 1) * npno], coef_ref[i, j].reshape(domain * pao, lanes)
            )
            out_ref[i, j] = total[:, npno:] * scale


def merge_into(takers, column_count, row_count, kept, got, target):
    col_place = lax.axis_index("col")
    away = jnp.bitwise_xor(lax.axis_index("row"), col_place * column_count // row_count)
    turn = col_place % len(takers)
    taken = functools.reduce(
        jnp.logical_or,
        [(turn == n) & (away == taker) for n, these in enumerate(takers) for taker in these],
    )

    @pl.when(taken)
    def _():
        target[...] = got[...]

    @pl.when(jnp.logical_not(taken))
    def _():
        target[...] = kept[...]


def merge_kernel(takers, column_count, row_count, kept_ref, got_ref, *refs):
    merge_into(takers, column_count, row_count, kept_ref, got_ref, refs[-1])


def one_column(takers, j, coef_ref, turned_ref, base_ref, factor_ref, held_ref, got_ref, scratch, store):
    row_count, column_count, domain, pao, lanes = coef_ref.shape
    npno = lanes // 2
    chunks = npno // 2
    packed_ref, metric_ref, wide_ref = scratch
    merge_into(takers, column_count, row_count, held_ref, got_ref, packed_ref)
    lows = [unpack(packed_ref[s], metric_ref.at[s]) for s in range(domain)]
    parts = []
    for s in range(domain):
        left = turned_ref[j, s]
        part = dot(left, metric_ref[s]) + left.astype(F32) * lows[s]
        parts.append(part.astype(BF16))
    product = jnp.concatenate(parts, axis=1)
    lane = lax.broadcasted_iota(jnp.int32, (chunks, lanes), 1)
    for i in range(row_count):
        wide_ref[i] = dot(
            product[i * npno : (i + 1) * npno], coef_ref[i, j].reshape(domain * pao, lanes)
        )
        even = wide_ref[i, pl.ds(0, chunks, 2), :]
        odd = wide_ref[i, pl.ds(1, chunks, 2), :]
        total = jnp.where(lane < npno, pltpu.roll(even, npno, 1), odd)
        store(i, base_ref[i, j] + factor_ref[i, j] * total)


def first_columns_kernel(takers, j, *refs):
    out_ref, scratch = refs[6], refs[7:]

    def store(i, value):
        out_ref[i] = value

    one_column(takers, j, *refs[:6], scratch, store)


def last_column_kernel(takers, *refs):
    row_count, column_count, _, _, lanes = refs[0].shape
    chunks = refs[2].shape[2]
    done = refs[6 : 5 + column_count]
    out_hbm, packed_ref, metric_ref, wide_ref, flat_ref, out_ref, sems = refs[5 + column_count :]

    def store(i, value):
        flat_ref[i, column_count - 1] = value
        for j in range(column_count - 1):
            flat_ref[i, j] = done[j][i]
        for q in range(chunks):
            out_ref[i, :, q * lanes : (q + 1) * lanes] = flat_ref[i, :, q, :]
        pltpu.make_async_copy(out_ref.at[i], out_hbm.at[i], sems.at[i]).start()

    one_column(takers, column_count - 1, *refs[:6], (packed_ref, metric_ref, wide_ref), store)
    for i in range(row_count):
        pltpu.make_async_copy(out_ref.at[i], out_hbm.at[i], sems.at[i]).wait()


def call(kernel, out_shape, in_specs, out_specs, scratch, name, flops, moved):
    return pl.pallas_call(
        kernel,
        out_shape=out_shape,
        in_specs=in_specs,
        out_specs=out_specs,
        scratch_shapes=scratch,
        compiler_params=pltpu.CompilerParams(vmem_limit_bytes=48 * 2**20),
        cost_estimate=pl.CostEstimate(flops=flops, bytes_accessed=moved, transcendentals=0),
        name=name,
    )


def neighbours(block, axis, other):
    size, rest = lax.axis_size(axis), lax.axis_size(other)
    even = lax.ppermute(block, axis, [(n, n ^ 1) for n in range(size)])
    pairs = [(n, n + 1) for n in range(1, size - 1, 2)]
    if axis == "row" and size == 2 * len(pairs) + 2 and all(a ^ b == 3 for a, b in pairs):
        return [even, lax.ppermute(block, axis, [(n, n ^ 3) for n in range(size)])]
    joint = pairs + [(b, a) for a, b in pairs]
    alone = [n for n in range(size) if n not in dict(joint)]
    route = [((m, a), (m, b)) for m in range(rest) for a, b in joint]
    trade = 1 if rest % 4 else 2
    route += [((m, a), (m ^ trade, a)) for m in range(rest) for a in alone]

    def place(m, n):
        return n * rest + m if axis == "row" else m * size + n

    return [even, lax.ppermute(block, ("row", "col"), [(place(*a), place(*b)) for a, b in route])]


def after(block, others):
    return call(
        pass_kernel,
        jax.ShapeDtypeStruct(block.shape, block.dtype),
        [VMEM] + [ANY] * len(others),
        VMEM,
        [],
        "after_others",
        0,
        0,
    )(block, *others)


def gather_metrics(packed, cores, units, first, second):
    order = ring_order(units)
    forward = [
        (order[n] * cores + k, order[(n + 1) % units] * cores + k)
        for n in range(units)
        for k in range(cores)
    ]
    backward = [(b, a) for a, b in forward]
    turns = [packed] + [None] * (units - 1)
    up = down = packed
    for step in range(1, units // 2 + 1):
        if step == 2 and first:
            up = after(up, first)
        up = lax.ppermute(up, "col", forward)
        if step == 2 and second:
            up = after(up, second)
        turns[step] = up
        if units - step > units // 2:
            down = lax.ppermute(down, "col", backward)
            turns[units - step] = down
    buffers = []
    for turn in turns:
        buffers.append(turn)
        for side in range(1, cores):
            swap = [
                (u * cores + k, u * cores + (k + side) % cores)
                for u in range(units)
                for k in range(cores)
            ]
            buffers.append(lax.ppermute(turn, "col", swap))
    return buffers


def spread(pieces, sources, column_count, row_count, first):
    rows, columns = lax.axis_size("row"), len(sources)
    bits = rows.bit_length() - 1
    assert rows == 1 << bits
    reached = [[0] for _ in range(bits)]
    for step in range(bits):
        pairs, takers = [], []
        for turn in range(bits):
            bit = 1 << ((turn + step) % bits)
            pairs += [
                (row * columns + c, (row ^ bit) * columns + c)
                for c in range(turn, columns, bits)
                for row in range(rows)
            ]
            takers.append([away ^ bit for away in reached[turn]])
            reached[turn] = reached[turn] + takers[turn]
        got = [lax.ppermute(piece, ("row", "col"), pairs) for piece in pieces]
        if step < bits - 1:
            pieces = [
                call(
                    functools.partial(merge_kernel, takers, column_count, row_count),
                    jax.ShapeDtypeStruct(piece.shape, piece.dtype),
                    [VMEM, VMEM] + [ANY] * len(others),
                    VMEM,
                    [],
                    "merge",
                    0,
                    0,
                )(piece, block, *others)
                for piece, block, others in zip(pieces, got, first)
            ]
    return pieces + got, takers


def on_device(
    fitting,
    coefficients,
    amplitudes,
    intersections,
    virtual_energy,
    occupied_energy,
    kept_count,
    orbital_atoms,
    fock_partner,
    fock_value,
):
    row_count, column_count = amplitudes.shape[:2]
    held, aux, pao = fitting.shape
    domain = orbital_atoms.shape[1]
    npno = virtual_energy.shape[2]
    terms = intersections.shape[2]
    columns = lax.axis_size("col")
    cores = row_count // column_count
    units = columns // cores
    scale = (2 * domain * aux) ** (-0.5)
    depth = pao + EXTRA
    half = pao // 2

    chunks = npno // 2
    lanes = 2 * npno
    atoms_table, fit, own_block, partner, value, occupied, virtual, coefs, inter, kept = [
        pltpu.with_memory_space_constraint(array, pltpu.HBM)
        for array in (
            orbital_atoms.T,
            fitting,
            amplitudes,
            fock_partner.T,
            fock_value.T,
            occupied_energy,
            virtual_energy,
            coefficients,
            intersections,
            kept_count.T,
        )
    ]
    packed, table, lines = call(
        pack_kernel,
        (
            jax.ShapeDtypeStruct((held, depth, half), BF16),
            jax.ShapeDtypeStruct(atoms_table.shape, jnp.int32),
            jax.ShapeDtypeStruct((row_count, column_count, chunks, lanes), BF16),
        ),
        [HBM] * 3,
        (VMEM,) * 3,
        [
            pltpu.VMEM(fitting.shape, BF16),
            pltpu.VMEM(amplitudes.shape, BF16),
            pltpu.VMEM((row_count, chunks, column_count, lanes), F32),
            pltpu.SemaphoreType.DMA((held,)),
            pltpu.SemaphoreType.DMA(()),
            pltpu.SemaphoreType.DMA(()),
        ],
        "pack_metric",
        2 * held * aux * pao * pao,
        fitting.size * 2,
    )(atoms_table, own_block, fit)
    row_halos = neighbours(lines, "row", "col")
    col_halos = neighbours(lines, "col", "row")
    shape = (row_count, column_count, domain, pao, lanes)
    own_coefficients, column_coefficients, own_turned, turned = call(
        prepare_kernel,
        (
            jax.ShapeDtypeStruct(shape, BF16),
            jax.ShapeDtypeStruct(shape, BF16),
            jax.ShapeDtypeStruct((row_count, domain, column_count * npno, pao), BF16),
            jax.ShapeDtypeStruct((column_count, domain, row_count * npno, pao), BF16),
        ),
        [HBM],
        (VMEM,) * 4,
        [pltpu.SemaphoreType.DMA((row_count,)), pltpu.SemaphoreType.DMA((row_count,))],
        "prepare",
        0,
        coefficients.size * 4,
    )(coefs)
    mats = jax.ShapeDtypeStruct((row_count, column_count, terms, npno, npno), BF16)
    flat = jax.ShapeDtypeStruct((row_count, column_count, chunks, lanes), F32)
    mats, turned_mats, factor = call(
        functools.partial(square_kernel, scale),
        (mats, mats, flat),
        [HBM] * 2,
        (VMEM,) * 3,
        [
            pltpu.VMEM(intersections.shape, BF16),
            pltpu.VMEM((column_count, chunks, terms, lanes), F32),
            pltpu.VMEM((column_count, terms, npno, lanes), F32),
            pltpu.SMEM(kept_count.shape[::-1], jnp.int32),
            pltpu.SemaphoreType.DMA((row_count,)),
            pltpu.SemaphoreType.DMA(()),
        ],
        "square",
        0,
        intersections.size * 4,
    )(kept, inter)
    buffers = gather_metrics(packed, cores, units, row_halos + [turned_mats], [own_turned])
    blocks = [lines] + row_halos + col_halos
    wanted = column_count * domain
    atoms = len(buffers) * held
    *pieces, metrics = call(
        functools.partial(select_kernel, cores, units),
        tuple(
            jax.ShapeDtypeStruct((n, depth, half), BF16) for n in [domain] * column_count + [atoms]
        ),
        [SMEM] + [VMEM] * len(buffers),
        (VMEM,) * (column_count + 1),
        [],
        "select_column_atoms",
        0,
        (wanted + 2 * atoms) * depth * half * 4,
    )(table, *buffers)
    exchange = call(
        functools.partial(row_kernel, cores, units, held, scale),
        jax.ShapeDtypeStruct((row_count, column_count, npno, npno), F32),
        [SMEM] + [VMEM] * 3,
        VMEM,
        [pltpu.VMEM((row_count * domain, pao, pao), BF16)],
        "row_exchange",
        2 * row_count * column_count * domain * pao * npno * (pao + npno),
        coefficients.size,
    )(table, own_coefficients, own_turned, metrics)

    sources = [c * column_count // row_count for c in range(columns)]
    first = [[exchange]] + [[]] * (column_count - 2) + [col_halos]
    pieces, takers = spread(pieces, sources, column_count, row_count, first)

    base = call(
        couple_kernel,
        flat,
        [HBM] * 4 + [VMEM] * (4 + len(blocks)),
        VMEM,
        [
            pltpu.VMEM((row_count * column_count, npno, lanes), F32),
            pltpu.VMEM((len(blocks) * row_count, column_count, npno, npno), BF16),
            pltpu.SMEM(fock_partner.shape[::-1], jnp.int32),
            pltpu.SMEM(fock_value.shape[::-1], F32),
            pltpu.SMEM(occupied_energy.shape, F32),
            pltpu.VMEM(virtual_energy.shape, F32),
            pltpu.SemaphoreType.DMA((4,)),
        ],
        "couple",
        4 * row_count * column_count * terms * npno**3,
        intersections.size * 4,
    )(partner, value, occupied, virtual, mats, turned_mats, factor, exchange, *blocks)

    scratch = [
        pltpu.VMEM((domain, depth, half), BF16),
        pltpu.VMEM((domain, pao, pao), BF16),
        pltpu.VMEM((row_count, npno, lanes), F32),
    ]
    cost = 2 * row_count * domain * pao * npno * (pao + npno)
    whole = (column_coefficients, turned, base, factor)
    done = [
        call(
            functools.partial(first_columns_kernel, takers, j),
            jax.ShapeDtypeStruct((row_count, chunks, lanes), F32),
            [VMEM] * 6,
            VMEM,
            scratch,
            "first_column",
            cost,
            coefficients.size,
        )(*whole, pieces[j], pieces[column_count + j])
        for j in range(column_count - 1)
    ]
    return call(
        functools.partial(last_column_kernel, takers),
        jax.ShapeDtypeStruct(amplitudes.shape, F32),
        [VMEM] * (5 + column_count),
        HBM,
        scratch
        + [
            pltpu.VMEM((row_count, column_count, chunks, lanes), F32),
            pltpu.VMEM(amplitudes.shape, F32),
            pltpu.SemaphoreType.DMA((row_count,)),
        ],
        "last_column",
        cost,
        coefficients.size,
    )(*whole, pieces[column_count - 1], pieces[-1], *done)


def solution(mesh):
    placed = (
        P(("row", "col"), None, None),
        P("row", "col", None, None, None),
        P("row", "col", None),
        P("row", "col", None, None),
        P("row", "col", None),
        P(),
        P("row", "col"),
        P(),
        P(),
        P(),
    )
    return jax.shard_map(
        on_device, mesh=mesh, in_specs=placed, out_specs=P("row", "col", None), check_vma=False
    )
```
